512 devices in a mesh: head: 16 (over x, y), seq: 32 (over z, core).
Axes of the slice: x: 4, y: 4, z: 16, core: 2. Of those that a mesh axis runs over, the one named last changes fastest.
Arguments:
- q_latent: bfloat16 [4096, 128, 512], P('seq', 'head'), may hold values from -14 to 14
- q_rope: bfloat16 [4096, 128, 64], P('seq', 'head'), may hold values from -4 to 4
- latent_cache: bfloat16 [16384, 512], P('seq'), may hold values from -4 to 4
- rope_keys: bfloat16 [16384, 64], P('seq'), may hold values from -4 to 4
- index_queries: bfloat16 [4096, 64, 128], P('seq', 'head'), may hold values from -6 to 6
- index_weights: float32 [4096, 64], P('seq', 'head'), may hold values from 0.05 to 0.4
- index_keys: bfloat16 [16384, 128], P('seq'), may hold values from -4 to 4
- sel_blocks: int32 [32, 16], replicated, may hold values from -1 to 127, as said below
Outputs:
- grad_index_queries: float32 [4096, 64, 128], P('seq', 'head')
- grad_index_weights: float32 [4096, 64], P('seq', 'head')
- grad_index_keys: float32 [16384, 128], P('seq')
The draws below stay inside these ranges and needn't reach their ends.
Inputs may be any that keep to these rules, and one draw needn't show every extreme that they name: `sel_blocks`: entry 0 of row d is 4 * d + 3. The other entries are distinct blocks no later than entry 0, never entry 0 itself, at most one of them from the key blocks 4 * e to 4 * e + 3 of any one e, followed by -1 entries; row d has exactly min(16, d + 2) entries that are not -1.
All inputs are finite; a program needn't handle non-finite values.
Results may differ from the reference program's by a relative error of at most 0.008.
Values may be sent and summed in bfloat16 or wider, within the bound.
No kernel may reach another device: no remote copies, remote signals or barrier semaphores. Data moves between devices by JAX's collectives and lax.ppermute only.
A program may use at most 64 MiB of HBM per device.

```python
import math
import jax
import jax.numpy as jnp
from jax import lax

H = 128
DL = 512
DR = 64
HI = 64
DI = 128
NSEL = 16
BLOCK = 128
KBLK_DEV = 4
SEQ = 16384
QTOKENS = 4096
N_SEQ = 32


def shared_normal(key, salt, shape):
    return jax.random.normal(jax.random.fold_in(key, salt), shape, jnp.float32)


def draw_latent_cache(key, part):
    raw = shared_normal(key, 101, (SEQ, DL))
    return jnp.clip(raw, -4.0, 4.0).astype(jnp.bfloat16)


def draw_index_keys(key, part):
    raw = shared_normal(key, 102, (SEQ, DI))
    return jnp.clip(raw, -4.0, 4.0).astype(jnp.bfloat16)


def draw_q_latent(key, part):
    own_key = jax.random.fold_in(key, 3)
    base = jax.random.normal(own_key, (N_SEQ * BLOCK, H, DL), jnp.float32)
    return jnp.clip(base, -4.0, 4.0).astype(jnp.bfloat16)


def draw_index_queries(key, part):
    own_key = jax.random.fold_in(key, 4)
    base = jax.random.normal(own_key, (N_SEQ * BLOCK, HI, DI), jnp.float32)
    return jnp.clip(base, -4.0, 4.0).astype(jnp.bfloat16)


def draw_sel_blocks(key, part):
    own_key = jax.random.fold_in(key, 5)
    score_key, local_key = jax.random.split(own_key)
    width = max(N_SEQ, NSEL - 1)
    device = jnp.arange(N_SEQ)[:, None]
    sources = jnp.arange(width)[None, :]
    ranking = jax.random.randint(score_key, (N_SEQ, width), 0, 1 << 20) * width + sources
    ranking = jnp.where(sources <= device, ranking, -1)
    best, which = lax.top_k(ranking, NSEL - 1)
    limit = jnp.where(which == device, KBLK_DEV - 1, KBLK_DEV)
    offsets = jax.random.randint(local_key, (N_SEQ, NSEL - 1), 0, limit)
    picked = jnp.where(best >= 0, which * KBLK_DEV + offsets, -1)
    own_block = device * KBLK_DEV + KBLK_DEV - 1
    return jnp.concatenate([own_block, picked], axis=1).astype(jnp.int32)


def block_levels(key, dims, pieces, low, largest):
    loudness = 1.0
    for axis_at, parts in pieces:
        draws = jax.random.uniform(jax.random.fold_in(jax.random.fold_in(key, 6), axis_at), (parts,), jnp.float32, low / len(pieces), largest / len(pieces))
        loudness = loudness * jnp.repeat(jnp.exp(draws), dims[axis_at] // parts).reshape((-1,) + (1,) * (len(dims) - 1 - axis_at))
    return loudness


def bell_draw(stream_key, shape, scale, reach, cuts=(), kind=jnp.bfloat16):
    drawn = jax.random.normal(stream_key, shape, jnp.float32) * scale
    if len(cuts) > 0:
        drawn = block_levels(stream_key, shape, cuts, -0.22, 0.18) * drawn
    return jnp.clip(drawn, min=-reach, max=reach).astype(kind)


def setup_inputs(seed: int = 0) -> dict:
    key_list = jax.random.split(jax.random.key(seed), 9)
    q_latent = draw_q_latent(jax.random.fold_in(key_list[8], 71), 0)
    q_rope = bell_draw(key_list[1], (QTOKENS, H, DR), 1.0, 4.0, ((0, 32), (1, 16)))
    latent_cache = draw_latent_cache(jax.random.fold_in(key_list[8], 71), 0)
    rope_keys = bell_draw(key_list[3], (SEQ, DR), 1.0, 4.0, ((0, 32),))
    index_queries = draw_index_queries(jax.random.fold_in(key_list[8], 71), 0)
    index_weights = jnp.clip(jnp.exp(math.log(0.4) - 2.0794415 * jax.random.uniform(key_list[5], (QTOKENS, HI), jnp.float32) ** block_levels(key_list[5], (QTOKENS, HI), ((0, 32), (1, 16)), -0.2, 0.2)), 0.05, 0.4)
    index_keys = draw_index_keys(jax.random.fold_in(key_list[8], 71), 0)
    sel_blocks = draw_sel_blocks(jax.random.fold_in(key_list[8], 71), 0)
    return {"q_latent": q_latent, "q_rope": q_rope, "latent_cache": latent_cache, "rope_keys": rope_keys, "index_queries": index_queries, "index_weights": index_weights, "index_keys": index_keys, "sel_blocks": sel_blocks}


score_scale = 192.0 ** (-0.5)
gelu_coef = math.sqrt(2.0 / math.pi)
cubic_coef = 0.044715

def gelu_pair(values):
    inner = gelu_coef * (values + cubic_coef * values * values * values)
    tangent = jnp.tanh(inner)
    active = 0.5 * values * (1.0 + tangent)
    slope = 0.5 * (1.0 + tangent) + 0.5 * values * (1.0 - tangent * tangent) * gelu_coef * (1.0 + 3.0 * cubic_coef * values * values)
    return (active, slope)

def head_probs(scores, key_mask):
    full_mask = key_mask[:, None]
    highest = lax.optimization_barrier(jnp.max(jnp.where(full_mask, scores, -jnp.inf), axis=(2, 3), keepdims=True))
    weights = jnp.where(full_mask, jnp.exp(scores - highest), 0.0)
    return lax.optimization_barrier(jnp.sum(weights / lax.optimization_barrier(jnp.sum(weights, axis=(2, 3), keepdims=True)), axis=1))

def logit_grad(target, logits, key_mask, loss_weight):
    highest = lax.optimization_barrier(jnp.max(jnp.where(key_mask, logits, -jnp.inf), axis=(1, 2), keepdims=True))
    weights = jnp.where(key_mask, jnp.exp(logits - highest), 0.0)
    predicted = weights / lax.optimization_barrier(jnp.sum(weights, axis=(1, 2), keepdims=True))
    return jnp.where(key_mask, loss_weight * (predicted - target), 0.0).astype(jnp.bfloat16)

def reference(q_latent, q_rope, latent_cache, rope_keys, index_queries, index_weights, index_keys, sel_blocks):
    block_total = SEQ // BLOCK
    latent_tables = latent_cache.reshape(block_total, BLOCK, DL)
    rope_tables = rope_keys.reshape(block_total, BLOCK, DR)
    index_tables = index_keys.reshape(block_total, BLOCK, DI)
    index_scale = DI ** (-0.5)
    loss_weight = float(NSEL * BLOCK)
    positions = jnp.arange(BLOCK)
    slots = jnp.arange(NSEL)

    def one_block(carry, inputs):
        lat_query, rope_query, idx_query, idx_weight, sel_row = inputs
        slot_valid = sel_row >= 0
        chosen_ids = jnp.where(slot_valid, sel_row, 0).astype(jnp.int32)
        sel_latent = jnp.take(latent_tables, chosen_ids, axis=0).astype(jnp.float32)
        sel_rope = jnp.take(rope_tables, chosen_ids, axis=0).astype(jnp.float32)
        sel_index = jnp.take(index_tables, chosen_ids, axis=0).astype(jnp.float32)
        key_mask = slot_valid[None, :, None] & ((slots[None, :, None] > 0) | (positions[None, None, :] <= positions[:, None, None]))
        scores = (jnp.einsum('thc,jkc->thjk', lat_query.astype(jnp.float32), sel_latent) + jnp.einsum('thc,jkc->thjk', rope_query.astype(jnp.float32), sel_rope)) * score_scale
        target = head_probs(scores, key_mask) / H
        pre = jnp.einsum('tid,jkd->tijk', idx_query.astype(jnp.float32), sel_index) * index_scale
        active, slope = gelu_pair(pre)
        logits = lax.optimization_barrier(jnp.sum(idx_weight[:, :, None, None] * active, axis=1))
        grad_logits = logit_grad(target, logits, key_mask, loss_weight).astype(jnp.float32)
        grad_weight = lax.optimization_barrier(jnp.sum(grad_logits[:, None] * active, axis=(2, 3)))
        grad_pre = (grad_logits[:, None] * idx_weight[:, :, None, None] * slope * index_scale).astype(jnp.bfloat16).astype(jnp.float32)
        grad_query = jnp.einsum('tijk,jkd->tid', grad_pre, sel_index)
        key_part = jnp.einsum('tijk,tid->jkd', grad_pre, idx_query.astype(jnp.float32))
        carry = carry.at[chosen_ids].add(key_part)
        return (carry, (grad_query, grad_weight))
    start = jnp.zeros((block_total, BLOCK, DI), jnp.float32)
    inputs = (q_latent.reshape(N_SEQ, BLOCK, H, DL), q_rope.reshape(N_SEQ, BLOCK, H, DR), index_queries.reshape(N_SEQ, BLOCK, HI, DI), index_weights.reshape(N_SEQ, BLOCK, HI), sel_blocks)
    key_grads, outputs = lax.scan(one_block, start, inputs)
    grad_queries = outputs[0].reshape(N_SEQ * BLOCK, HI, DI)
    grad_weights = outputs[1].reshape(N_SEQ * BLOCK, HI)
    return (grad_queries, grad_weights, key_grads.reshape(SEQ, DI))
```

```python
import math

import jax
import jax.numpy as jnp
from jax import lax
from jax.sharding import PartitionSpec as P

score_scale = 192.0 ** (-0.5)
gelu_coef = math.sqrt(2.0 / math.pi)
cubic_coef = 0.044715
bf16 = jnp.bfloat16
f32 = jnp.float32


def gelu_pair(values):
    inner = gelu_coef * (values + cubic_coef * values * values * values)
    tangent = jnp.tanh(inner)
    active = 0.5 * values * (1.0 + tangent)
    slope = 0.5 * (1.0 + tangent) + 0.5 * values * (1.0 - tangent * tangent) * gelu_coef * (
        1.0 + 3.0 * cubic_coef * values * values
    )
    return (active, slope)


def exchange(array, axis):
    return lax.all_to_all(array, axis, split_axis=0, concat_axis=0, tiled=True)


def pad_lanes(array, width):
    return jnp.pad(array, [(0, 0)] * (array.ndim - 1) + [(0, width - array.shape[-1])])


def body(
    q_latent, q_rope, latent_cache, rope_keys, index_queries, index_weights, index_keys, sel_blocks
):
    head_count = lax.axis_size("head")
    seq_count = lax.axis_size("seq")
    head_index = lax.axis_index("head")
    seq_index = lax.axis_index("seq")
    block, heads, latent_width = q_latent.shape
    rope_width = q_rope.shape[2]
    index_heads, index_width = index_queries.shape[1:]
    slot_count = sel_blocks.shape[1]
    local_blocks = latent_cache.shape[0] // block
    index_scale = index_width ** (-0.5)
    loss_weight = float(slot_count * block)
    groups = head_count // 2
    rows = block // groups
    small = rows // 2
    tokens = block // head_count
    half_width = latent_width // 2
    lanes = half_width + index_width
    remote_slots = slot_count - 1
    group = head_index % groups
    half = head_index // groups

    later = sel_blocks[:, 1:]
    offsets = later - seq_index * local_blocks
    inside = (later >= 0) & (offsets >= 0) & (offsets < local_blocks)
    wanted = jnp.any(inside, axis=1)
    which = jnp.sum(jnp.where(inside, offsets, 0), axis=1)
    sel_row = lax.dynamic_index_in_dim(sel_blocks, seq_index, 0, keepdims=False)
    slot_valid = sel_row >= 0
    source = jnp.where(slot_valid, sel_row // local_blocks, 0)

    latent_tables = latent_cache.reshape(local_blocks, block, latent_width)
    rope_tables = rope_keys.reshape(local_blocks, block, rope_width)
    index_tables = index_keys.reshape(local_blocks, block, index_width)
    first_row = group * rows
    latent_share = lax.dynamic_slice(
        latent_tables, (0, first_row, half * half_width), (local_blocks, rows, half_width)
    )
    index_share = lax.dynamic_slice(
        index_tables, (0, first_row, 0), (local_blocks, rows, index_width)
    )
    rope_share = lax.dynamic_slice(rope_tables, (0, first_row, 0), (local_blocks, rows, rope_width))
    share = jnp.concatenate(
        [latent_share, jnp.where(half == 0, index_share, pad_lanes(rope_share, index_width))],
        axis=-1,
    )
    packed = jnp.broadcast_to(share[0], (seq_count, rows, lanes))
    for k in range(1, local_blocks):
        packed = jnp.where((which == k)[:, None, None], share[k], packed)
    fetched = exchange(packed, "seq")
    chosen = jnp.take(fetched, source[1:], axis=0).reshape(remote_slots * rows, lanes)

    share_rows = remote_slots * rows
    query_rows = tokens * heads
    index_rows = tokens * index_heads
    latent_parts = q_latent.reshape(head_count, query_rows, latent_width)
    rope_parts = q_rope.reshape(head_count, query_rows, rope_width)
    index_parts = index_queries.reshape(head_count, index_rows, index_width)
    weight_parts = index_weights.reshape(head_count, index_rows, 1)
    high = lax.reduce_precision(weight_parts, 8, 7)
    middle = lax.reduce_precision(weight_parts - high, 8, 7)
    low = weight_parts - high - middle
    weight_pieces = pad_lanes(
        jnp.concatenate([high, middle, low], axis=-1).astype(bf16), index_width
    )
    second = jnp.concatenate(
        [
            latent_parts[:, :, lanes:],
            pad_lanes(rope_parts, 128),
            jnp.concatenate([index_parts, weight_pieces], axis=1),
        ],
        axis=-1,
    )
    outgoing = jnp.concatenate(
        [
            jnp.broadcast_to(chosen, (head_count, share_rows, lanes)),
            latent_parts[:, :, :lanes],
            second,
        ],
        axis=1,
    )
    arrived = exchange(outgoing, "head")

    key_low = arrived[:groups, :share_rows].reshape(groups * share_rows, lanes)
    key_high = arrived[groups:, :share_rows].reshape(groups * share_rows, lanes)
    query_first = arrived[:, share_rows : share_rows + query_rows]
    query_second = arrived[:, share_rows + query_rows :]
    queries = jnp.concatenate(
        [query_first, query_second[:, :, : 128 + rope_width]], axis=-1
    )
    index_q = query_second[:, :index_rows, 256:]
    weights = jnp.sum(query_second[:, index_rows:, 256:259].astype(f32), axis=-1)
    own = slice((local_blocks - 1) * block, local_blocks * block)
    own_index = index_keys[own]
    remote_keys = jnp.concatenate(
        [
            key_low[:, :half_width],
            key_high[:, :half_width],
            key_high[:, half_width : half_width + rope_width],
        ],
        axis=-1,
    )
    own_keys = jnp.concatenate([latent_cache[own], rope_keys[own]], axis=-1)
    keys = jnp.concatenate([remote_keys, own_keys], axis=0)
    index_k = jnp.concatenate([key_low[:, half_width:], own_index], axis=0)
    total = keys.shape[0]

    token_at = head_index * tokens + jnp.arange(tokens)
    remote_mask = jnp.broadcast_to(
        slot_valid[None, 1:, None], (groups, remote_slots, rows)
    ).reshape(-1)
    key_mask = jnp.concatenate(
        [
            jnp.broadcast_to(remote_mask, (tokens, remote_mask.shape[0])),
            jnp.arange(block)[None, :] <= token_at[:, None],
        ],
        axis=1,
    )

    scores = (
        jnp.einsum("sqc,kc->sqk", queries, keys, preferred_element_type=f32) * score_scale
    ).reshape(head_count, tokens, heads, total)
    mask = key_mask[None, :, None, :]
    highest = jnp.max(jnp.where(mask, scores, -jnp.inf), axis=-1, keepdims=True)
    powers = jnp.where(mask, jnp.exp(scores - highest), 0.0)
    target = jnp.sum(powers / jnp.sum(powers, axis=-1, keepdims=True), axis=(0, 2)) / (
        heads * head_count
    )

    pre = (
        jnp.einsum("sqc,kc->sqk", index_q, index_k, preferred_element_type=f32) * index_scale
    ).reshape(head_count, tokens, index_heads, total)
    active, slope = gelu_pair(pre)
    weights = weights.reshape(head_count, tokens, index_heads, 1)
    logits = jnp.sum(weights * active, axis=(0, 2))
    top = jnp.max(jnp.where(key_mask, logits, -jnp.inf), axis=-1, keepdims=True)
    likely = jnp.where(key_mask, jnp.exp(logits - top), 0.0)
    predicted = likely / jnp.sum(likely, axis=-1, keepdims=True)
    grad_logits = jnp.where(key_mask, loss_weight * (predicted - target), 0.0).astype(bf16)
    grad_float = grad_logits.astype(f32)[None, :, None, :]
    grad_weights = jnp.sum(grad_float * active, axis=-1)
    grad_pre = (
        (grad_float * weights * slope * index_scale)
        .astype(bf16)
        .reshape(head_count, index_rows, total)
    )
    grad_queries = jnp.einsum("sqk,kc->sqc", grad_pre, index_k, preferred_element_type=f32)
    key_part = jnp.einsum("sqk,sqc->kc", grad_pre, index_q, preferred_element_type=f32)

    remote_part = key_part[: groups * share_rows].reshape(
        groups, remote_slots, 2, small, index_width
    )
    own_part = key_part[groups * share_rows :].reshape(groups, 1, 2, small, index_width)
    shares = (
        jnp.concatenate([own_part, remote_part], axis=1)
        .transpose(2, 0, 1, 3, 4)
        .reshape(head_count, slot_count * small, index_width)
        .astype(bf16)
    )
    summed = jnp.sum(exchange(shares, "head").astype(f32), axis=0).reshape(
        slot_count, small, index_width
    )
    found = (source[1:][None, :] == jnp.arange(seq_count)[:, None]) & slot_valid[1:][None, :]
    slot_of = jnp.sum(jnp.where(found, jnp.arange(1, slot_count)[None, :], 0), axis=1)
    returned = exchange(jnp.take(summed, slot_of, axis=0), "seq")
    owner = wanted[:, None] & (which[:, None] == jnp.arange(local_blocks)[None, :])
    owned = jnp.sum(
        jnp.where(owner[:, :, None, None], returned[:, None], 0.0), axis=0
    )
    owned = owned.at[local_blocks - 1].add(summed[0])

    own_rows = local_blocks * small
    last = jnp.concatenate(
        [
            jnp.broadcast_to(
                owned.reshape(own_rows, index_width), (head_count, own_rows, index_width)
            ),
            grad_queries,
            pad_lanes(grad_weights.reshape(head_count, 1, index_rows), index_width),
            jnp.zeros((head_count, 7, index_width), f32),
        ],
        axis=1,
    )
    final = exchange(last, "head")
    grad_keys = (
        final[:, :own_rows]
        .reshape(2, groups, local_blocks, small, index_width)
        .transpose(2, 1, 0, 3, 4)
        .reshape(local_blocks * block, index_width)
    )
    out_queries = final[:, own_rows : own_rows + index_rows].reshape(
        block, index_heads, index_width
    )
    out_weights = final[:, own_rows + index_rows, :index_rows].reshape(block, index_heads)
    return (out_queries, out_weights, grad_keys)


def solution(mesh):
    placed = (
        P("seq", "head", None),
        P("seq", "head", None),
        P("seq", None),
        P("seq", None),
        P("seq", "head", None),
        P("seq", "head"),
        P("seq", None),
        P(),
    )
    return jax.shard_map(
        body,
        mesh=mesh,
        in_specs=placed,
        out_specs=(P("seq", "head", None), P("seq", "head"), P("seq", None)),
        check_vma=False,
    )
```

```python
import functools
import math

import jax
import jax.numpy as jnp
from jax import lax
from jax.experimental import pallas as pl
from jax.experimental.pallas import tpu as pltpu
from jax.sharding import PartitionSpec as P

score_scale = 192.0 ** (-0.5)
gelu_coef = math.sqrt(2.0 / math.pi)
cubic_coef = 0.044715
bf16 = jnp.bfloat16
f32 = jnp.float32


def dot_last(a, b):
    return lax.dot_general(a, b, (((1,), (1,)), ((), ())), preferred_element_type=f32)


def dot(a, b, precision=None):
    return jnp.dot(a, b, preferred_element_type=f32, precision=precision)


def gelu_pair(values):
    square = values * values
    tangent = jnp.tanh(values * (gelu_coef + (gelu_coef * cubic_coef) * square))
    upper = 0.5 + 0.5 * tangent
    active = values * upper
    slope = upper + active * (1.0 - upper) * (
        2.0 * gelu_coef + (6.0 * gelu_coef * cubic_coef) * square
    )
    return (active, slope)


def first_kernel(
    groups, sel_turned, latent, rope_turned, index, packed, wide, narrow, turned, rope, sems
):
    slots, destinations = sel_turned.shape
    local_blocks, rows, latent_width = wide.shape
    block = latent.shape[0] // local_blocks
    half_width = latent_width // 2
    head = lax.axis_index("head")
    group = lax.rem(head, groups)
    is_low = head < groups
    copies = [pltpu.make_async_copy(rope_turned, turned, sems.at[0])]
    spots = []
    for k in range(local_blocks):
        at = pl.ds(pl.multiple_of(k * block + group * rows, rows), rows)
        spots.append(at)
        copies.append(pltpu.make_async_copy(latent.at[at], wide.at[k], sems.at[1 + 2 * k]))
        copies.append(pltpu.make_async_copy(index.at[at], narrow.at[k], sems.at[2 + 2 * k]))
    for copy in copies:
        copy.start()

    total = packed.shape[0]
    repeat = lax.broadcasted_iota(jnp.int32, (total, destinations), 0) // rows
    repeat = (repeat == lax.broadcasted_iota(jnp.int32, (total, destinations), 1)).astype(f32)
    chosen = dot_last(repeat, sel_turned[...].astype(f32))
    offset = chosen - (lax.axis_index("seq") * local_blocks).astype(f32)
    slot = lax.broadcasted_iota(jnp.int32, (total, slots), 1)
    inside = (chosen >= 0) & (offset >= 0) & (offset < local_blocks) & (slot > 0)
    which = jnp.sum(jnp.where(inside, offset, 0.0), axis=1, keepdims=True)
    width = local_blocks * rows
    row = lax.broadcasted_iota(jnp.int32, (total, width), 0) % rows
    column = lax.broadcasted_iota(jnp.int32, (total, width), 1)
    pick = (column.astype(f32) == which * rows + row.astype(f32)).astype(bf16)

    for copy in copies:
        copy.wait()
    rope_rows = turned[...].astype(f32)
    rope[...] = jnp.concatenate([rope_rows, rope_rows], axis=0).T.astype(bf16)
    parts = []
    for k in range(local_blocks):
        parts.append(
            jnp.concatenate(
                [
                    jnp.where(is_low, wide[k, :, 0:half_width], wide[k, :, half_width:]),
                    jnp.where(is_low, narrow[k], rope[spots[k], :]),
                ],
                axis=1,
            )
        )
    share = jnp.concatenate(parts, axis=0)
    packed[...] = dot(pick, share).astype(bf16)


def second_kernel(local_blocks, sel, fetched, latent, rope, index, weight, outgoing):
    destinations = outgoing.shape[0]
    slots = sel.shape[0]
    rows, lanes = fetched.shape[1:]
    here = lax.axis_index("seq")
    query_rows = latent.shape[0] // destinations
    index_rows = index.shape[0] // destinations
    rope_rows = rope.shape[0] // destinations
    weight_rows = weight.shape[0] // destinations
    first = (slots - 1) * rows
    second = first + query_rows
    tall = index_rows + weight_rows
    rest = query_rows - tall
    for j in range(1, slots):
        source = lax.div(jnp.maximum(sel[j, here], 0), local_blocks)
        piece = fetched[source]
        for k in range(destinations):
            outgoing[k, (j - 1) * rows : j * rows, :] = piece
    for k in range(destinations):
        at = k * query_rows
        outgoing[k, first:second, :] = latent[at : at + query_rows, 0:lanes]
        outgoing[k, second : second + tall, 0:128] = latent[at : at + tall, lanes:]
        outgoing[k, second : second + rest, 128:256] = latent[
            at + tall : at + query_rows, lanes:
        ]
        outgoing[k, second + rest : second + tall, 128:256] = rope[
            k * rope_rows : (k + 1) * rope_rows, :
        ]
        outgoing[k, second : second + index_rows, 256:384] = index[
            k * index_rows : (k + 1) * index_rows, :
        ]
        outgoing[k, second + index_rows : second + tall, 256:384] = weight[
            k * weight_rows : (k + 1) * weight_rows, :
        ]


def compute_kernel(
    share_rows,
    loss_weight,
    index_scale,
    arrived,
    bias,
    key_bias,
    own_latent,
    own_rope,
    own_index,
    grad_queries,
    grad_weights,
    shares,
    keys,
    index_k,
    scores,
    highest,
    active,
    slope,
    grad_pre,
    logit_rows,
    target_rows,
    grad_keys,
):
    sources, _, lanes = arrived.shape
    groups = sources // 2
    tokens, total = bias.shape
    block, latent_width = own_latent.shape
    half_width = latent_width // 2
    index_width = own_index.shape[1]
    query_rows = target_rows.shape[0]
    heads = query_rows // tokens
    index_rows = logit_rows.shape[0]
    index_heads = index_rows // tokens
    remote = groups * share_rows
    tile = 2 * 128
    tiles = total // tile
    step = 4
    score_rows = step * query_rows
    index_step = step
    chunk = index_step * index_rows
    first = share_rows
    second = share_rows + query_rows

    low = arrived[0:groups, 0:share_rows, :]
    high = arrived[groups:sources, 0:share_rows, :]
    keys[0:remote, 0:half_width] = low[:, :, 0:half_width].reshape(remote, half_width)
    index_k[0:remote, :] = low[:, :, half_width:lanes].reshape(remote, index_width)
    keys[0:remote, half_width : latent_width + 128] = high.reshape(remote, lanes)
    keys[remote:total, 0:latent_width] = own_latent[...]
    keys[remote:total, latent_width : latent_width + 128] = own_rope[...]
    index_k[remote:total, :] = own_index[...]
    keys[:, latent_width + 128 :] = key_bias[...]
    target_rows[...] = jnp.zeros_like(target_rows)
    logit_rows[...] = jnp.zeros_like(logit_rows)

    lane_low = lax.broadcasted_iota(jnp.int32, (query_rows // 2, 128), 1) < 64
    lane_low = lane_low.astype(f32)
    keep_low = lane_low.astype(bf16)[None]
    keep_high = (1.0 - lane_low).astype(bf16)[None]
    tall = arrived.shape[1] - second
    rest = query_rows - tall

    on_token = (
        lax.broadcasted_iota(jnp.int32, (query_rows, 128), 0) // heads
        == lax.broadcasted_iota(jnp.int32, (query_rows, 128), 1)
    ).astype(bf16)
    on_token = jnp.broadcast_to(on_token[None], (step, query_rows, 128))

    def weight_of(c):
        pieces = arrived[
            pl.ds(c * index_step, index_step), second + index_rows : second + tall, 256:384
        ].astype(f32)
        early = lax.broadcasted_iota(jnp.int32, pieces.shape, 2) < 3
        return jnp.concatenate(
            [
                jnp.sum(jnp.where(early, pieces, 0.0), axis=-1, keepdims=True),
                jnp.sum(jnp.where(early, 0.0, pieces), axis=-1, keepdims=True),
            ],
            axis=1,
        )

    @pl.loop(0, sources // step)
    def _(c):
        here = pl.ds(c * step, step)
        score_at = pl.ds(pl.multiple_of(c * score_rows, score_rows), score_rows)
        rows = pl.ds(pl.multiple_of(c * chunk, chunk), chunk)
        rope = arrived[here, second + rest : second + tall, 128:256]
        queries = jnp.concatenate(
            [
                arrived[here, first:second, :],
                jnp.concatenate(
                    [
                        arrived[here, second : second + tall, 0:128],
                        arrived[here, second : second + rest, 128:256],
                    ],
                    axis=1,
                ),
                jnp.concatenate([rope * keep_low, rope * keep_high], axis=1),
                on_token,
            ],
            axis=-1,
        ).reshape(score_rows, latent_width + 256)
        index_q = arrived[here, second : second + index_rows, 256:384].reshape(chunk, index_width)
        weights = weight_of(c)
        best = jnp.full((score_rows, 128), -3e38, f32)
        for k in range(tiles):
            at = slice(k * tile, (k + 1) * tile)
            part = dot_last(queries, keys[at, :])
            scores[score_at, at] = part
            best = jnp.maximum(best, jnp.maximum(part[:, 0:128], part[:, 128:256]))
            act, rate = gelu_pair(dot_last(index_q, index_k[at, :]) * index_scale)
            active[rows, at] = act
            slope[rows, at] = rate
            logit_rows[:, at] += jnp.sum(
                act.reshape(index_step, index_rows, tile) * weights, axis=0
            )
        highest[score_at, :] = best

    @pl.loop(0, sources // step)
    def _(c):
        score_at = pl.ds(pl.multiple_of(c * score_rows, score_rows), score_rows)
        top = jnp.max(highest[score_at, :], axis=1, keepdims=True)
        sums = jnp.zeros((score_rows, 128), f32)
        for k in range(tiles):
            at = slice(k * tile, (k + 1) * tile)
            power = jnp.exp((scores[score_at, at] - top) * score_scale)
            scores[score_at, at] = power
            sums = sums + (power[:, 0:128] + power[:, 128:256])
        weight = 1.0 / ((heads * sources) * jnp.sum(sums, axis=1, keepdims=True))
        weight = weight.reshape(step, query_rows, 1)
        for k in range(tiles):
            at = slice(k * tile, (k + 1) * tile)
            power = scores[score_at, at].reshape(step, query_rows, tile)
            target_rows[:, at] += jnp.sum(power * weight, axis=0)

    def gather(count):
        return (
            lax.broadcasted_iota(jnp.int32, (tokens, tokens * count), 1) // count
            == lax.broadcasted_iota(jnp.int32, (tokens, tokens * count), 0)
        ).astype(f32)

    spread = (
        lax.broadcasted_iota(jnp.int32, (index_rows, tokens), 0) // index_heads
        == lax.broadcasted_iota(jnp.int32, (index_rows, tokens), 1)
    ).astype(bf16)
    logits = dot(gather(index_heads), logit_rows[...], lax.Precision.HIGHEST) + bias[...]
    target = dot(gather(heads), target_rows[...], lax.Precision.HIGHEST)
    likely = jnp.exp(logits - jnp.max(logits, axis=1, keepdims=True))
    predicted = likely / jnp.sum(likely, axis=1, keepdims=True)
    grad_logits = jnp.where(
        bias[...] == 0.0, loss_weight * (predicted - target), 0.0
    ).astype(bf16)
    logit_rows[...] = dot(spread, grad_logits)

    @pl.loop(0, sources // index_step)
    def _(c):
        rows = pl.ds(pl.multiple_of(c * chunk, chunk), chunk)
        weights = weight_of(c) * index_scale
        sums = jnp.zeros((chunk, 128), f32)
        for k in range(tiles):
            at = slice(k * tile, (k + 1) * tile)
            grad = logit_rows[:, at][None]
            product = (
                active[rows, at].reshape(index_step, index_rows, tile) * grad
            ).reshape(chunk, tile)
            sums = sums + (product[:, 0:128] + product[:, 128:256])
            grad_pre[rows, at] = (
                (slope[rows, at].reshape(index_step, index_rows, tile) * (grad * weights))
                .reshape(chunk, tile)
                .astype(bf16)
            )
        turned = jnp.broadcast_to(jnp.sum(sums, axis=1, keepdims=True), (chunk, 128)).T
        turned = turned[0:8]
        turned_high = turned.astype(bf16)
        turned_low = (turned - turned_high.astype(f32)).astype(bf16)
        for i in range(index_step):
            grad_weights[c * index_step + i] = jnp.concatenate([turned_high, turned_low], axis=0)

    grad_queries[...] = dot(grad_pre[...], index_k[...]).astype(bf16)
    turned = (
        arrived[:, second : second + index_rows, 256:384]
        .reshape(sources * index_rows, index_width)
        .astype(f32)
        .T.astype(bf16)
    )
    for k in range(tiles):
        at = slice(k * tile, (k + 1) * tile)
        grad_keys[at, :] = dot(turned, grad_pre[:, at]).T
    small = block // sources
    slots = total // block
    for g in range(groups):
        own = grad_keys[remote + g * 2 * small : remote + (g + 1) * 2 * small, :]
        own = own.reshape(1, 2, small, index_width)
        rest_keys = grad_keys[g * share_rows : (g + 1) * share_rows, :]
        rest_keys = rest_keys.reshape(slots - 1, 2, small, index_width)
        both_keys = jnp.concatenate([own, rest_keys], axis=0)
        for i in range(2):
            shares[i * groups + g] = both_keys[:, i].reshape(block, index_width).astype(bf16)


def last_kernel(groups, index_heads, final, grad_queries, grad_weights, grad_keys):
    sources, _, width = final.shape
    block = grad_weights.shape[1]
    tokens = block // sources
    index_rows = tokens * index_heads
    local_blocks = grad_keys.shape[0] // block
    small = block // sources
    own_rows = local_blocks * small
    second = own_rows + index_rows
    for k in range(sources):
        part = final[k, 0:own_rows, :].astype(f32)
        half, group = k // groups, k % groups
        for j in range(local_blocks):
            at = j * block + group * 2 * small + half * small
            grad_keys[at : at + small, :] = part[j * small : (j + 1) * small]
        grad_queries[k * index_rows : (k + 1) * index_rows, :] = final[
            k, own_rows:second, :
        ].astype(f32)
    together = 128 // index_rows
    first_lane = lax.rem(lax.axis_index("head"), together) * index_rows
    row = lax.broadcasted_iota(jnp.int32, (block, width), 0)
    lane = lax.broadcasted_iota(jnp.int32, (block, width), 1)
    spot = lane - first_lane
    keep = (spot >= 0) & (spot < index_rows) & (lax.div(spot, index_heads) == row % tokens)
    which = lax.broadcasted_iota(jnp.int32, (8, width), 0)
    head = lax.rem(lax.broadcasted_iota(jnp.int32, (8, width), 1), index_heads)
    fold = (which == head).astype(bf16)
    result = jnp.zeros((8, block), f32)
    for i in range(2):
        lines = []
        for k in range(sources):
            whole = final[k, second : second + 16, :].astype(f32)
            lines.append(jnp.broadcast_to(whole[8 * i : 8 * i + 1], (tokens, width)))
        lines = jnp.concatenate(lines, axis=0)
        result = result + dot_last(fold, jnp.where(keep, lines, 0.0).astype(bf16))
    grad_weights[...] = result[0:index_heads]


def exchange(array, axis):
    return lax.all_to_all(array, axis, split_axis=0, concat_axis=0, tiled=True)


def exchange_alone(array, axis, others):
    array, others = lax.optimization_barrier((array, others))
    return lax.optimization_barrier((exchange(array, axis), others))


def pad_lanes(array, width):
    return jnp.pad(array, [(0, 0)] * (array.ndim - 1) + [(0, width - array.shape[-1])])


def body(
    q_latent, q_rope, latent_cache, rope_keys, index_queries, index_weights, index_keys, sel_blocks
):
    head_count = lax.axis_size("head")
    seq_count = lax.axis_size("seq")
    head_index = lax.axis_index("head")
    seq_index = lax.axis_index("seq")
    block, heads, latent_width = q_latent.shape
    rope_width = q_rope.shape[2]
    index_heads, index_width = index_queries.shape[1:]
    slot_count = sel_blocks.shape[1]
    local_blocks = latent_cache.shape[0] // block
    index_scale = index_width ** (-0.5)
    loss_weight = float(slot_count * block)
    groups = head_count // 2
    rows = block // groups
    small = rows // 2
    tokens = block // head_count
    half_width = latent_width // 2
    lanes = half_width + index_width
    remote_slots = slot_count - 1

    later = sel_blocks[:, 1:]
    offsets = later - seq_index * local_blocks
    inside = (later >= 0) & (offsets >= 0) & (offsets < local_blocks)
    wanted = jnp.any(inside, axis=1)
    which = jnp.sum(jnp.where(inside, offsets, 0), axis=1)
    sel_row = lax.dynamic_index_in_dim(sel_blocks, seq_index, 0, keepdims=False)
    slot_valid = sel_row >= 0
    source = jnp.where(slot_valid, sel_row // local_blocks, 0)
    in_vmem = pl.BlockSpec(memory_space=pltpu.VMEM)
    in_smem = pl.BlockSpec(memory_space=pltpu.SMEM)
    in_place = pl.BlockSpec(memory_space=pl.ANY)

    packed = pl.pallas_call(
        functools.partial(first_kernel, groups),
        out_shape=jax.ShapeDtypeStruct((seq_count * rows, lanes), bf16),
        in_specs=[in_vmem] + [in_place] * 3,
        out_specs=in_vmem,
        scratch_shapes=[
            pltpu.VMEM((local_blocks, rows, latent_width), bf16),
            pltpu.VMEM((local_blocks, rows, index_width), bf16),
            pltpu.VMEM((rope_width, local_blocks * block), bf16),
            pltpu.VMEM((local_blocks * block, 2 * rope_width), bf16),
            pltpu.SemaphoreType.DMA((1 + 2 * local_blocks,)),
        ],
        compiler_params=pltpu.CompilerParams(vmem_limit_bytes=60 * 1024 * 1024),
    )(sel_blocks.T, latent_cache, rope_keys.T, index_keys)
    fetched = exchange(packed.reshape(seq_count, rows, lanes), "seq")

    share_rows = remote_slots * rows
    query_rows = tokens * heads
    index_rows = tokens * index_heads
    latent_parts = q_latent.reshape(block * heads, latent_width)
    rope_parts = q_rope.reshape(head_count, 2, query_rows // 2, rope_width)
    rope_parts = jnp.concatenate([rope_parts[:, 0], rope_parts[:, 1]], axis=-1)
    rope_parts = rope_parts.reshape(head_count * query_rows // 2, 2 * rope_width)
    index_parts = index_queries.reshape(head_count * index_rows, index_width)
    weight_parts = index_weights.reshape(head_count, 2, index_rows // 2, 1)
    high = lax.reduce_precision(weight_parts, 8, 7)
    middle = lax.reduce_precision(weight_parts - high, 8, 7)
    low = weight_parts - high - middle
    pieces = jnp.concatenate([high, middle, low], axis=-1).astype(bf16)
    pieces = pad_lanes(jnp.concatenate([pieces[:, 0], pieces[:, 1]], axis=-1), 128)
    pieces = pieces.reshape(head_count * index_rows // 2, 128)
    packed_rows = share_rows + query_rows + index_rows + index_rows // 2
    own = slice((local_blocks - 1) * block, local_blocks * block)
    own_rope = jnp.concatenate([rope_keys[own], rope_keys[own]], axis=-1)
    total = slot_count * block
    token_at = head_index * tokens + jnp.arange(tokens)
    remote_mask = jnp.broadcast_to(
        slot_valid[None, 1:, None], (groups, remote_slots, rows)
    ).reshape(-1)
    key_mask = jnp.concatenate(
        [
            jnp.broadcast_to(remote_mask, (tokens, remote_mask.shape[0])),
            jnp.arange(block)[None, :] <= token_at[:, None],
        ],
        axis=1,
    )
    bias = jnp.where(key_mask, 0.0, -1e30).astype(f32)
    key_bias = pad_lanes(bias.T.astype(bf16), 128)
    outgoing = pl.pallas_call(
        functools.partial(second_kernel, local_blocks),
        out_shape=jax.ShapeDtypeStruct((head_count, packed_rows, lanes), bf16),
        in_specs=[in_smem] + [in_vmem] * 5,
        out_specs=in_vmem,
        compiler_params=pltpu.CompilerParams(vmem_limit_bytes=24 * 1024 * 1024),
    )(sel_blocks.T, fetched, latent_parts, rope_parts, index_parts, pieces)
    found = (source[1:][None, :] == jnp.arange(seq_count)[:, None]) & slot_valid[1:][None, :]
    slot_of = jnp.sum(jnp.where(found, jnp.arange(1, slot_count)[None, :], 0), axis=1)
    owner = wanted[:, None] & (which[:, None] == jnp.arange(local_blocks)[None, :])
    owner = owner.astype(f32)
    arrived, (bias, key_bias, own_latent, own_rope, own_index, slot_of, owner) = exchange_alone(
        outgoing,
        "head",
        (bias, key_bias, latent_cache[own], own_rope, index_keys[own], slot_of, owner),
    )

    all_rows = head_count * index_rows
    grad_queries, grad_weights, shares = pl.pallas_call(
        functools.partial(compute_kernel, share_rows, loss_weight, index_scale),
        out_shape=(
            jax.ShapeDtypeStruct((all_rows, index_width), bf16),
            jax.ShapeDtypeStruct((head_count, 16, 128), bf16),
            jax.ShapeDtypeStruct((head_count, slot_count * small, index_width), bf16),
        ),
        in_specs=[in_vmem] * 6,
        out_specs=(in_vmem, in_vmem, in_vmem),
        scratch_shapes=[
            pltpu.VMEM((total, latent_width + 256), bf16),
            pltpu.VMEM((total, index_width), bf16),
            pltpu.VMEM((head_count * query_rows, total), f32),
            pltpu.VMEM((head_count * query_rows, 128), f32),
            pltpu.VMEM((all_rows, total), f32),
            pltpu.VMEM((all_rows, total), f32),
            pltpu.VMEM((all_rows, total), bf16),
            pltpu.VMEM((index_rows, total), f32),
            pltpu.VMEM((query_rows, total), f32),
            pltpu.VMEM((total, index_width), f32),
        ],
        compiler_params=pltpu.CompilerParams(vmem_limit_bytes=36 * 1024 * 1024),
    )(arrived, bias, key_bias, own_latent, own_rope, own_index)

    collected, (grad_queries, grad_weights, slot_of, owner) = exchange_alone(
        shares, "head", (grad_queries, grad_weights, slot_of, owner)
    )
    summed = jnp.sum(collected.astype(f32), axis=0).reshape(slot_count, small, index_width)
    own_sum = summed[0]
    returned, (own_sum, grad_queries, grad_weights, owner) = exchange_alone(
        jnp.take(summed, slot_of, axis=0).astype(bf16),
        "seq",
        (own_sum, grad_queries, grad_weights, owner),
    )
    owned = jnp.sum(owner[:, :, None, None] * returned.astype(f32)[:, None], axis=0)
    owned = owned.at[local_blocks - 1].add(own_sum)

    own_rows = local_blocks * small
    last = jnp.concatenate(
        [
            jnp.broadcast_to(
                owned.reshape(own_rows, index_width).astype(bf16), (head_count, own_rows, index_width)
            ),
            grad_queries.reshape(head_count, index_rows, index_width),
            grad_weights,
        ],
        axis=1,
    )
    final, _ = exchange_alone(last, "head", ())
    out_queries, out_weights, grad_keys = pl.pallas_call(
        functools.partial(last_kernel, groups, index_heads),
        out_shape=(
            jax.ShapeDtypeStruct((block * index_heads, index_width), f32),
            jax.ShapeDtypeStruct((index_heads, block), f32),
            jax.ShapeDtypeStruct((local_blocks * block, index_width), f32),
        ),
        in_specs=[in_vmem],
        out_specs=(in_vmem, in_vmem, in_vmem),
        compiler_params=pltpu.CompilerParams(vmem_limit_bytes=16 * 1024 * 1024),
    )(final)
    return (out_queries.reshape(block, index_heads, index_width), out_weights.T, grad_keys)


def solution(mesh):
    placed = (
        P("seq", "head", None),
        P("seq", "head", None),
        P("seq", None),
        P("seq", None),
        P("seq", "head", None),
        P("seq", "head"),
        P("seq", None),
        P(),
    )
    return jax.shard_map(
        body,
        mesh=mesh,
        in_specs=placed,
        out_specs=(P("seq", "head", None), P("seq", "head"), P("seq", None)),
        check_vma=False,
    )
```

```python
import functools
import math

import jax
import jax.numpy as jnp
from jax import lax
from jax.experimental import pallas as pl
from jax.experimental.pallas import tpu as pltpu
from jax.sharding import PartitionSpec as P

score_scale = 192.0 ** (-0.5)
gelu_coef = math.sqrt(2.0 / math.pi)
cubic_coef = 0.044715
bf16 = jnp.bfloat16
f32 = jnp.float32


def dot_last(a, b):
    return lax.dot_general(a, b, (((1,), (1,)), ((), ())), preferred_element_type=f32)


def dot(a, b, precision=None):
    return jnp.dot(a, b, preferred_element_type=f32, precision=precision)


def gelu_pair(values):
    square = values * values
    tangent = jnp.tanh(values * (gelu_coef + (gelu_coef * cubic_coef) * square))
    upper = 0.5 + 0.5 * tangent
    active = values * upper
    slope = upper + active * (1.0 - upper) * (
        2.0 * gelu_coef + (6.0 * gelu_coef * cubic_coef) * square
    )
    return (active, slope)


def first_kernel(
    groups, sel_turned, latent, rope_turned, index, packed, own_rope, wide, narrow, turned, rope, sems
):
    slots, destinations = sel_turned.shape
    local_blocks, rows, latent_width = wide.shape
    block = latent.shape[0] // local_blocks
    half_width = latent_width // 2
    head = lax.axis_index("head")
    group = lax.rem(head, groups)
    is_low = head < groups
    copies = [pltpu.make_async_copy(rope_turned, turned, sems.at[0])]
    spots = []
    for k in range(local_blocks):
        at = pl.ds(pl.multiple_of(k * block + group * rows, rows), rows)
        spots.append(at)
        copies.append(pltpu.make_async_copy(latent.at[at], wide.at[k], sems.at[1 + 2 * k]))
        copies.append(pltpu.make_async_copy(index.at[at], narrow.at[k], sems.at[2 + 2 * k]))
    for copy in copies:
        copy.start()

    total = packed.shape[0]
    repeat = lax.broadcasted_iota(jnp.int32, (total, destinations), 0) // rows
    repeat = (repeat == lax.broadcasted_iota(jnp.int32, (total, destinations), 1)).astype(f32)
    chosen = dot_last(repeat, sel_turned[...].astype(f32))
    offset = chosen - (lax.axis_index("seq") * local_blocks).astype(f32)
    slot = lax.broadcasted_iota(jnp.int32, (total, slots), 1)
    inside = (chosen >= 0) & (offset >= 0) & (offset < local_blocks) & (slot > 0)
    which = jnp.sum(jnp.where(inside, offset, 0.0), axis=1, keepdims=True)
    width = local_blocks * rows
    row = lax.broadcasted_iota(jnp.int32, (total, width), 0) % rows
    column = lax.broadcasted_iota(jnp.int32, (total, width), 1)
    pick = (column.astype(f32) == which * rows + row.astype(f32)).astype(bf16)

    for copy in copies:
        copy.wait()
    rope_rows = turned[...].astype(f32)
    rope[...] = jnp.concatenate([rope_rows, rope_rows], axis=0).T.astype(bf16)
    parts = []
    for k in range(local_blocks):
        parts.append(
            jnp.concatenate(
                [
                    jnp.where(is_low, wide[k, :, 0:half_width], wide[k, :, half_width:]),
                    jnp.where(is_low, narrow[k], rope[spots[k], :]),
                ],
                axis=1,
            )
        )
    own_rope[...] = rope[(local_blocks - 1) * block :, :]
    share = jnp.concatenate(parts, axis=0)
    packed[...] = dot(pick, share).astype(bf16)


def place(side):
    head = lax.axis_index("head")
    core = lax.rem(lax.axis_index("seq"), 2)
    x, y = lax.div(head, side), lax.rem(head, side)
    return core, jnp.where(core == 0, y, x), jnp.where(core == 0, x, y)


def head_at(side, core, u, v):
    return jnp.where(core == 0, v * side + u, u * side + v)


def query_kernel(
    side, groups, sel_turned, latent, rope, index, weight, out0, out1, out2, out3, bias, key_bias
):
    outs = (out0, out1, out2, out3)
    chunks = side * side
    slots, destinations = sel_turned.shape
    query_rows = latent.shape[0] // chunks
    lanes = out0.shape[2]
    index_rows = index.shape[0] // chunks
    rope_rows = rope.shape[0] // chunks
    weight_rows = weight.shape[0] // chunks
    tall = index_rows + weight_rows
    rest = query_rows - tall
    core, u, _ = place(side)
    for k in range(side):
        out = outs[k]
        for v in range(side):
            chunk = head_at(side, core, lax.rem(u + k, side), v)

            def at(count, size, begin=0):
                return pl.ds(pl.multiple_of(chunk * count + begin, 16), size)

            out[v, 0:query_rows, :] = latent[at(query_rows, query_rows), 0:lanes]
            out[v, query_rows : query_rows + tall, 0:128] = latent[at(query_rows, tall), lanes:]
            out[v, query_rows : query_rows + rest, 128:256] = latent[
                at(query_rows, rest, tall), lanes:
            ]
            out[v, query_rows + rest : query_rows + tall, 128:256] = rope[
                at(rope_rows, rope_rows), :
            ]
            out[v, query_rows : query_rows + index_rows, 256:384] = index[
                at(index_rows, index_rows), :
            ]
            out[v, query_rows + index_rows : query_rows + tall, 256:384] = weight[
                at(weight_rows, weight_rows), :
            ]
    tokens, total = bias.shape
    rows = total // slots // groups
    share_rows = (slots - 1) * rows
    remote = groups * share_rows
    here = lax.axis_index("seq")
    head = lax.axis_index("head")
    table = sel_turned[...].astype(f32)
    pick = lax.broadcasted_iota(jnp.int32, (tokens, destinations), 1) == here
    valid = (dot_last(pick.astype(f32), table) >= 0).astype(f32)
    key = lax.broadcasted_iota(jnp.int32, (slots, total), 1)
    slot = lax.div(lax.rem(key, share_rows), rows) + 1
    mark = (slot == lax.broadcasted_iota(jnp.int32, (slots, total), 0)).astype(f32)
    key = lax.broadcasted_iota(jnp.int32, (tokens, total), 1)
    token = lax.broadcasted_iota(jnp.int32, (tokens, total), 0) + head * tokens
    good = ((key < remote) & (dot(valid, mark) > 0)) | ((key >= remote) & (key - remote <= token))
    masks = jnp.where(good, 0.0, -1e30)
    bias[...] = masks
    tall_masks = jnp.concatenate([masks, jnp.zeros((128 - tokens, total), f32)], axis=0)
    key_bias[...] = tall_masks.T.astype(bf16)


def stage_kernel(local_blocks, sel, fetched, in0, in1, in2, in3, outgoing):
    parts = (in0, in1, in2, in3)
    slots = sel.shape[0]
    rows = fetched.shape[1]
    height = in0.shape[1]
    here = lax.axis_index("seq")
    first = (slots - 1) * rows
    for j in range(1, slots):
        piece = fetched[lax.div(jnp.maximum(sel[j, here], 0), local_blocks)]
        for v in range(len(parts)):
            outgoing[v, (j - 1) * rows : j * rows, :] = piece
    for k in range(len(parts)):
        for v in range(len(parts)):
            at = first + k * height
            outgoing[v, at : at + height, :] = parts[k][v]


def spread_kernel(staged, outgoing):
    side, height, _ = outgoing.shape
    share = height // side
    for v in range(side):
        piece = staged[v, 0:share, :]
        for u in range(side):
            outgoing[u, v * share : (v + 1) * share, :] = piece


def compute_kernel(
    loss_weight,
    index_scale,
    index_heads,
    staged,
    spread_shares,
    bias,
    key_bias,
    own_rope,
    latent,
    index,
    grad_queries,
    grad_weights,
    shares,
    keys,
    index_k,
    scores,
    highest,
    active,
    slope,
    grad_pre,
    logit_rows,
    target_rows,
    grad_keys,
    sems,
):
    sources, share_rows, lanes = spread_shares.shape
    step = staged.shape[0]
    groups = sources // 2
    tokens, total = bias.shape
    block = own_rope.shape[0]
    latent_width = latent.shape[1]
    half_width = latent_width // 2
    index_width = index.shape[1]
    query_rows = target_rows.shape[0]
    heads = query_rows // tokens
    index_rows = logit_rows.shape[0]
    remote = groups * share_rows
    tile = 2 * 128
    tiles = total // tile
    score_rows = step * query_rows
    chunk = step * index_rows
    height = (staged.shape[1] - share_rows) // step
    tall = height - query_rows
    rest = query_rows - tall
    core, own_u, _ = place(step)
    own_rows = pl.ds(latent.shape[0] - block, block)
    copies = (
        pltpu.make_async_copy(
            latent.at[own_rows], keys.at[pl.ds(remote, block), pl.ds(0, latent_width)], sems.at[0]
        ),
        pltpu.make_async_copy(index.at[own_rows], index_k.at[pl.ds(remote, block)], sems.at[1]),
    )
    for copy in copies:
        copy.start()

    for g in range(groups):
        at = slice(g * share_rows, (g + 1) * share_rows)
        x, y = g // step, g % step
        low = jnp.where(core == 0, y * step + x, x * step + y)
        x = x + step // 2
        high = jnp.where(core == 0, y * step + x, x * step + y)
        keys[at, 0:half_width] = spread_shares[low, :, 0:half_width]
        index_k[at, :] = spread_shares[low, :, half_width:]
        keys[at, half_width : latent_width + 128] = spread_shares[high]
    keys[remote:total, latent_width : latent_width + 128] = own_rope[...]
    keys[:, latent_width + 128 :] = key_bias[...]
    target_rows[...] = jnp.zeros_like(target_rows)
    logit_rows[...] = jnp.zeros_like(logit_rows)
    for copy in copies:
        copy.wait()

    lane_low = lax.broadcasted_iota(jnp.int32, (query_rows // 2, 128), 1) < 64
    lane_low = lane_low.astype(f32)
    keep_low = lane_low.astype(bf16)
    keep_high = (1.0 - lane_low).astype(bf16)

    on_token = (
        lax.broadcasted_iota(jnp.int32, (query_rows, 128), 0) // heads
        == lax.broadcasted_iota(jnp.int32, (query_rows, 128), 1)
    ).astype(bf16)

    def queries_of(v):
        pieces = []
        for k in range(step):
            at = share_rows + k * height
            below = at + query_rows
            rope = staged[v, below + rest : below + tall, 128:256]
            pieces.append(
                jnp.concatenate(
                    [
                        staged[v, at:below, :],
                        jnp.concatenate(
                            [
                                staged[v, below : below + tall, 0:128],
                                staged[v, below : below + rest, 128:256],
                            ],
                            axis=0,
                        ),
                        jnp.concatenate([rope * keep_low, rope * keep_high], axis=0),
                        on_token,
                    ],
                    axis=1,
                )
            )
        return jnp.concatenate(pieces, axis=0)

    def index_queries_of(v):
        pieces = []
        for k in range(step):
            below = share_rows + k * height + query_rows
            pieces.append(staged[v, below : below + index_rows, 256:384])
        return jnp.concatenate(pieces, axis=0)

    def weights_of(v):
        columns = []
        for k in range(step):
            below = share_rows + k * height + query_rows
            pieces = staged[v, below + index_rows : below + tall, 256:384].astype(f32)
            early = lax.broadcasted_iota(jnp.int32, pieces.shape, 1) < 3
            columns.append(jnp.sum(jnp.where(early, pieces, 0.0), axis=1, keepdims=True))
            columns.append(jnp.sum(jnp.where(early, 0.0, pieces), axis=1, keepdims=True))
        return jnp.concatenate(columns, axis=0).reshape(step, index_rows, 1)

    def source_of(v, k):
        return head_at(step, core, lax.rem(own_u + step - k, step), v)

    @pl.loop(0, sources // step)
    def _(c):
        score_at = pl.ds(pl.multiple_of(c * score_rows, score_rows), score_rows)
        rows = pl.ds(pl.multiple_of(c * chunk, chunk), chunk)
        queries = queries_of(c)
        index_q = index_queries_of(c)
        weights = weights_of(c)
        best = jnp.full((score_rows, 128), -3e38, f32)
        for k in range(tiles):
            at = slice(k * tile, (k + 1) * tile)
            part = dot_last(queries, keys[at, :])
            scores[score_at, at] = part
            best = jnp.maximum(best, jnp.maximum(part[:, 0:128], part[:, 128:256]))
            act, rate = gelu_pair(dot_last(index_q, index_k[at, :]) * index_scale)
            active[rows, at] = act
            slope[rows, at] = rate
            logit_rows[:, at] += jnp.sum(
                act.reshape(step, index_rows, tile) * weights, axis=0
            )
        highest[score_at, :] = best

    @pl.loop(0, sources // step)
    def _(c):
        score_at = pl.ds(pl.multiple_of(c * score_rows, score_rows), score_rows)
        top = jnp.max(highest[score_at, :], axis=1, keepdims=True)
        sums = jnp.zeros((score_rows, 128), f32)
        for k in range(tiles):
            at = slice(k * tile, (k + 1) * tile)
            power = jnp.exp((scores[score_at, at] - top) * score_scale)
            scores[score_at, at] = power
            sums = sums + (power[:, 0:128] + power[:, 128:256])
        weight = 1.0 / ((heads * sources) * jnp.sum(sums, axis=1, keepdims=True))
        weight = weight.reshape(step, query_rows, 1)
        for k in range(tiles):
            at = slice(k * tile, (k + 1) * tile)
            power = scores[score_at, at].reshape(step, query_rows, tile)
            target_rows[:, at] += jnp.sum(power * weight, axis=0)

    def gather(count):
        return (
            lax.broadcasted_iota(jnp.int32, (tokens, tokens * count), 1) // count
            == lax.broadcasted_iota(jnp.int32, (tokens, tokens * count), 0)
        ).astype(f32)

    spread = (
        lax.broadcasted_iota(jnp.int32, (index_rows, tokens), 0) // index_heads
        == lax.broadcasted_iota(jnp.int32, (index_rows, tokens), 1)
    ).astype(bf16)
    logits = dot(gather(index_heads), logit_rows[...], lax.Precision.HIGHEST) + bias[...]
    target = dot(gather(heads), target_rows[...], lax.Precision.HIGHEST)
    likely = jnp.exp(logits - jnp.max(logits, axis=1, keepdims=True))
    predicted = likely / jnp.sum(likely, axis=1, keepdims=True)
    grad_logits = jnp.where(
        bias[...] == 0.0, loss_weight * (predicted - target), 0.0
    ).astype(bf16)
    logit_rows[...] = dot(spread, grad_logits)

    @pl.loop(0, sources // step)
    def _(c):
        rows = pl.ds(pl.multiple_of(c * chunk, chunk), chunk)
        weights = weights_of(c) * index_scale
        sums = jnp.zeros((chunk, 128), f32)
        for k in range(tiles):
            at = slice(k * tile, (k + 1) * tile)
            grad = logit_rows[:, at][None]
            product = (
                active[rows, at].reshape(step, index_rows, tile) * grad
            ).reshape(chunk, tile)
            sums = sums + (product[:, 0:128] + product[:, 128:256])
            grad_pre[rows, at] = (
                (slope[rows, at].reshape(step, index_rows, tile) * (grad * weights))
                .reshape(chunk, tile)
                .astype(bf16)
            )
        turned = jnp.broadcast_to(jnp.sum(sums, axis=1, keepdims=True), (chunk, 128)).T
        for k in range(step):
            own = turned[0:8] if k == 0 else pltpu.roll(turned[0:8], 128 - k * index_rows, 1)
            own_high = own.astype(bf16)
            own_low = (own - own_high.astype(f32)).astype(bf16)
            grad_weights[source_of(c, k)] = jnp.concatenate([own_high, own_low], axis=0)

    result = dot(grad_pre[...], index_k[...]).astype(bf16)
    for v in range(step):
        for k in range(step):
            at = (v * step + k) * index_rows
            grad_queries[source_of(v, k)] = result[at : at + index_rows]
    turned = jnp.concatenate([index_queries_of(v) for v in range(step)], axis=0)
    turned = turned.astype(f32).T.astype(bf16)
    for k in range(tiles):
        at = slice(k * tile, (k + 1) * tile)
        grad_keys[at, :] = dot(turned, grad_pre[:, at]).T
    small = block // sources
    slots = total // block
    for g in range(groups):
        own = grad_keys[remote + g * 2 * small : remote + (g + 1) * 2 * small, :]
        own = own.reshape(1, 2, small, index_width)
        rest_keys = grad_keys[g * share_rows : (g + 1) * share_rows, :]
        rest_keys = rest_keys.reshape(slots - 1, 2, small, index_width)
        both_keys = jnp.concatenate([own, rest_keys], axis=0)
        for i in range(2):
            shares[i * groups + g] = both_keys[:, i].reshape(block, index_width).astype(bf16)


def last_kernel(groups, index_heads, final, grad_queries, grad_weights, grad_keys):
    sources, _, width = final.shape
    block = grad_weights.shape[1]
    tokens = block // sources
    index_rows = tokens * index_heads
    local_blocks = grad_keys.shape[0] // block
    small = block // sources
    own_rows = local_blocks * small
    second = own_rows + index_rows
    for k in range(sources):
        part = final[k, 0:own_rows, :].astype(f32)
        half, group = k // groups, k % groups
        for j in range(local_blocks):
            at = j * block + group * 2 * small + half * small
            grad_keys[at : at + small, :] = part[j * small : (j + 1) * small]
        grad_queries[k * index_rows : (k + 1) * index_rows, :] = final[
            k, own_rows:second, :
        ].astype(f32)
    row = lax.broadcasted_iota(jnp.int32, (block, width), 0)
    lane = lax.broadcasted_iota(jnp.int32, (block, width), 1)
    keep = (lane < index_rows) & (lax.div(lane, index_heads) == row % tokens)
    which = lax.broadcasted_iota(jnp.int32, (8, width), 0)
    head = lax.rem(lax.broadcasted_iota(jnp.int32, (8, width), 1), index_heads)
    fold = (which == head).astype(bf16)
    result = jnp.zeros((8, block), f32)
    for i in range(2):
        lines = []
        for k in range(sources):
            whole = final[k, second : second + 16, :].astype(f32)
            lines.append(jnp.broadcast_to(whole[8 * i : 8 * i + 1], (tokens, width)))
        lines = jnp.concatenate(lines, axis=0)
        result = result + dot_last(fold, jnp.where(keep, lines, 0.0).astype(bf16))
    grad_weights[...] = result[0:index_heads]


def exchange(array, axis, groups=None):
    return lax.all_to_all(
        array, axis, split_axis=0, concat_axis=0, tiled=True, axis_index_groups=groups
    )


def exchange_alone(array, axis, others, groups=None):
    array, others = lax.optimization_barrier((array, others))
    return lax.optimization_barrier((exchange(array, axis, groups), others))


def flat_index(side, seq_count, u, v, seq):
    x, y = (v, u) if seq % 2 == 0 else (u, v)
    return (x * side + y) * seq_count + seq


def lines(side, seq_count, along_u):
    return [
        [
            flat_index(side, seq_count, *((i, j) if along_u else (j, i)), seq)
            for i in range(side)
        ]
        for seq in range(seq_count)
        for j in range(side)
    ]


def shift_along_u(side, seq_count, k):
    return [
        (
            flat_index(side, seq_count, u, v, seq),
            flat_index(side, seq_count, (u + k) % side, v, seq),
        )
        for seq in range(seq_count)
        for u in range(side)
        for v in range(side)
    ]


def pad_lanes(array, width):
    return jnp.pad(array, [(0, 0)] * (array.ndim - 1) + [(0, width - array.shape[-1])])


def body(
    q_latent, q_rope, latent_cache, rope_keys, index_queries, index_weights, index_keys, sel_blocks
):
    head_count = lax.axis_size("head")
    seq_count = lax.axis_size("seq")
    head_index = lax.axis_index("head")
    seq_index = lax.axis_index("seq")
    block, heads, latent_width = q_latent.shape
    rope_width = q_rope.shape[2]
    index_heads, index_width = index_queries.shape[1:]
    slot_count = sel_blocks.shape[1]
    local_blocks = latent_cache.shape[0] // block
    index_scale = index_width ** (-0.5)
    loss_weight = float(slot_count * block)
    groups = head_count // 2
    side = math.isqrt(head_count)
    rows = block // groups
    small = rows // 2
    tokens = block // head_count
    half_width = latent_width // 2
    lanes = half_width + index_width
    remote_slots = slot_count - 1

    later = sel_blocks[:, 1:]
    offsets = later - seq_index * local_blocks
    inside = (later >= 0) & (offsets >= 0) & (offsets < local_blocks)
    wanted = jnp.any(inside, axis=1)
    which = jnp.sum(jnp.where(inside, offsets, 0), axis=1)
    sel_row = lax.dynamic_index_in_dim(sel_blocks, seq_index, 0, keepdims=False)
    slot_valid = sel_row >= 0
    source = jnp.where(slot_valid, sel_row // local_blocks, 0)
    in_vmem = pl.BlockSpec(memory_space=pltpu.VMEM)
    in_smem = pl.BlockSpec(memory_space=pltpu.SMEM)
    in_place = pl.BlockSpec(memory_space=pl.ANY)

    packed, own_rope = pl.pallas_call(
        functools.partial(first_kernel, groups),
        out_shape=(
            jax.ShapeDtypeStruct((seq_count * rows, lanes), bf16),
            jax.ShapeDtypeStruct((block, 2 * rope_width), bf16),
        ),
        in_specs=[in_vmem] + [in_place] * 3,
        out_specs=(in_vmem, in_vmem),
        scratch_shapes=[
            pltpu.VMEM((local_blocks, rows, latent_width), bf16),
            pltpu.VMEM((local_blocks, rows, index_width), bf16),
            pltpu.VMEM((rope_width, local_blocks * block), bf16),
            pltpu.VMEM((local_blocks * block, 2 * rope_width), bf16),
            pltpu.SemaphoreType.DMA((1 + 2 * local_blocks,)),
        ],
        compiler_params=pltpu.CompilerParams(vmem_limit_bytes=60 * 1024 * 1024),
    )(sel_blocks.T, latent_cache, rope_keys.T, index_keys)
    fetched = exchange(packed.reshape(seq_count, rows, lanes), "seq")

    share_rows = remote_slots * rows
    query_rows = tokens * heads
    index_rows = tokens * index_heads
    latent_parts = q_latent.reshape(block * heads, latent_width)
    rope_parts = q_rope.reshape(head_count, 2, query_rows // 2, rope_width)
    rope_parts = jnp.concatenate([rope_parts[:, 0], rope_parts[:, 1]], axis=-1)
    rope_parts = rope_parts.reshape(head_count * query_rows // 2, 2 * rope_width)
    index_parts = index_queries.reshape(head_count * index_rows, index_width)
    weight_parts = index_weights.reshape(head_count, 2, index_rows // 2, 1)
    high = lax.reduce_precision(weight_parts, 8, 7)
    middle = lax.reduce_precision(weight_parts - high, 8, 7)
    low = weight_parts - high - middle
    pieces = jnp.concatenate([high, middle, low], axis=-1).astype(bf16)
    pieces = pad_lanes(jnp.concatenate([pieces[:, 0], pieces[:, 1]], axis=-1), 128)
    pieces = pieces.reshape(head_count * index_rows // 2, 128)
    height = query_rows + index_rows + index_rows // 2
    total = slot_count * block
    axes = ("head", "seq")
    *parts, bias, key_bias = pl.pallas_call(
        functools.partial(query_kernel, side, groups),
        out_shape=tuple([jax.ShapeDtypeStruct((side, height, lanes), bf16)] * side)
        + (
            jax.ShapeDtypeStruct((tokens, total), f32),
            jax.ShapeDtypeStruct((total, 128), bf16),
        ),
        in_specs=[in_vmem] * 5,
        out_specs=tuple([in_vmem] * (side + 2)),
        compiler_params=pltpu.CompilerParams(vmem_limit_bytes=24 * 1024 * 1024),
    )(sel_blocks.T, latent_parts, rope_parts, index_parts, pieces)
    for k in range(1, side):
        parts[k] = lax.ppermute(parts[k], axes, shift_along_u(side, seq_count, k))
    outgoing = pl.pallas_call(
        functools.partial(stage_kernel, local_blocks),
        out_shape=jax.ShapeDtypeStruct((side, share_rows + side * height, lanes), bf16),
        in_specs=[in_smem] + [in_vmem] * (side + 1),
        out_specs=in_vmem,
        compiler_params=pltpu.CompilerParams(vmem_limit_bytes=24 * 1024 * 1024),
    )(sel_blocks.T, fetched, *parts)
    found = (source[1:][None, :] == jnp.arange(seq_count)[:, None]) & slot_valid[1:][None, :]
    slot_of = jnp.sum(jnp.where(found, jnp.arange(1, slot_count)[None, :], 0), axis=1)
    owner = wanted[:, None] & (which[:, None] == jnp.arange(local_blocks)[None, :])
    owner = owner.astype(f32)
    later = (bias, key_bias, own_rope, slot_of, owner)
    staged, later = exchange_alone(outgoing, axes, later, lines(side, seq_count, False))
    spread = pl.pallas_call(
        spread_kernel,
        out_shape=jax.ShapeDtypeStruct((side, side * share_rows, lanes), bf16),
        in_specs=[in_vmem],
        out_specs=in_vmem,
        compiler_params=pltpu.CompilerParams(vmem_limit_bytes=16 * 1024 * 1024),
    )(staged)
    spread, (staged, bias, key_bias, own_rope, slot_of, owner) = exchange_alone(
        spread, axes, (staged, *later), lines(side, seq_count, True)
    )

    all_rows = head_count * index_rows
    grad_queries, grad_weights, shares = pl.pallas_call(
        functools.partial(compute_kernel, loss_weight, index_scale, index_heads),
        out_shape=(
            jax.ShapeDtypeStruct((head_count, index_rows, index_width), bf16),
            jax.ShapeDtypeStruct((head_count, 16, 128), bf16),
            jax.ShapeDtypeStruct((head_count, slot_count * small, index_width), bf16),
        ),
        in_specs=[in_vmem] * 5 + [in_place] * 2,
        out_specs=(in_vmem, in_vmem, in_vmem),
        scratch_shapes=[
            pltpu.VMEM((total, latent_width + 256), bf16),
            pltpu.VMEM((total, index_width), bf16),
            pltpu.VMEM((head_count * query_rows, total), f32),
            pltpu.VMEM((head_count * query_rows, 128), f32),
            pltpu.VMEM((all_rows, total), f32),
            pltpu.VMEM((all_rows, total), f32),
            pltpu.VMEM((all_rows, total), bf16),
            pltpu.VMEM((index_rows, total), f32),
            pltpu.VMEM((query_rows, total), f32),
            pltpu.VMEM((total, index_width), f32),
            pltpu.SemaphoreType.DMA((2,)),
        ],
        compiler_params=pltpu.CompilerParams(vmem_limit_bytes=36 * 1024 * 1024),
    )(
        staged,
        spread.reshape(head_count, share_rows, lanes),
        bias,
        key_bias,
        own_rope,
        latent_cache,
        index_keys,
    )

    collected, (grad_queries, grad_weights, slot_of, owner) = exchange_alone(
        shares, "head", (grad_queries, grad_weights, slot_of, owner)
    )
    summed = jnp.sum(collected.astype(f32), axis=0).reshape(slot_count, small, index_width)
    own_sum = summed[0]
    returned, (own_sum, grad_queries, grad_weights, owner) = exchange_alone(
        jnp.take(summed, slot_of, axis=0).astype(bf16),
        "seq",
        (own_sum, grad_queries, grad_weights, owner),
    )
    owned = jnp.sum(owner[:, :, None, None] * returned.astype(f32)[:, None], axis=0)
    owned = owned.at[local_blocks - 1].add(own_sum)

    own_rows = local_blocks * small
    last = jnp.concatenate(
        [
            jnp.broadcast_to(
                owned.reshape(own_rows, index_width).astype(bf16), (head_count, own_rows, index_width)
            ),
            grad_queries,
            grad_weights,
        ],
        axis=1,
    )
    final, _ = exchange_alone(last, "head", ())
    out_queries, out_weights, grad_keys = pl.pallas_call(
        functools.partial(last_kernel, groups, index_heads),
        out_shape=(
            jax.ShapeDtypeStruct((block * index_heads, index_width), f32),
            jax.ShapeDtypeStruct((index_heads, block), f32),
            jax.ShapeDtypeStruct((local_blocks * block, index_width), f32),
        ),
        in_specs=[in_vmem],
        out_specs=(in_vmem, in_vmem, in_vmem),
        compiler_params=pltpu.CompilerParams(vmem_limit_bytes=16 * 1024 * 1024),
    )(final)
    return (out_queries.reshape(block, index_heads, index_width), out_weights.T, grad_keys)


def solution(mesh):
    placed = (
        P("seq", "head", None),
        P("seq", "head", None),
        P("seq", None),
        P("seq", None),
        P("seq", "head", None),
        P("seq", "head"),
        P("seq", None),
        P(),
    )
    return jax.shard_map(
        body,
        mesh=mesh,
        in_specs=placed,
        out_specs=(P("seq", "head", None), P("seq", "head"), P("seq", None)),
        check_vma=False,
    )
```

```python
import functools
import math

import jax
import jax.numpy as jnp
from jax import lax
from jax.experimental import pallas as pl
from jax.experimental.pallas import tpu as pltpu
from jax.sharding import PartitionSpec as P

score_scale = 192.0 ** (-0.5)
gelu_coef = math.sqrt(2.0 / math.pi)
cubic_coef = 0.044715
bf16 = jnp.bfloat16
f32 = jnp.float32


def dot_last(a, b):
    return lax.dot_general(a, b, (((1,), (1,)), ((), ())), preferred_element_type=f32)


def dot(a, b, precision=None):
    return jnp.dot(a, b, preferred_element_type=f32, precision=precision)


def gelu_pair(values):
    square = values * values
    tangent = jnp.tanh(values * (gelu_coef + (gelu_coef * cubic_coef) * square))
    upper = 0.5 + 0.5 * tangent
    active = values * upper
    slope = upper + active * (1.0 - upper) * (
        2.0 * gelu_coef + (6.0 * gelu_coef * cubic_coef) * square
    )
    return (active, slope)


def first_kernel(
    groups,
    sel_turned,
    latent,
    rope_turned,
    index,
    packed,
    own_rope,
    wide,
    narrow,
    turned,
    rope,
    table,
    sems,
):
    slots, destinations = sel_turned.shape
    local_blocks, rows, latent_width = wide.shape
    block = latent.shape[0] // local_blocks
    half_width = latent_width // 2
    head = lax.axis_index("head")
    group = lax.rem(head, groups)
    is_low = head < groups
    last = 1 + 2 * local_blocks
    copies = [pltpu.make_async_copy(rope_turned, turned, sems.at[0])]
    table_copy = pltpu.make_async_copy(sel_turned, table, sems.at[last])
    table_copy.start()
    spots = []
    for k in range(local_blocks):
        at = pl.ds(pl.multiple_of(k * block + group * rows, rows), rows)
        spots.append(at)
        copies.append(pltpu.make_async_copy(latent.at[at], wide.at[k], sems.at[1 + 2 * k]))
        copies.append(pltpu.make_async_copy(index.at[at], narrow.at[k], sems.at[2 + 2 * k]))
    for copy in copies:
        copy.start()

    total = packed.shape[0]
    repeat = lax.broadcasted_iota(jnp.int32, (total, destinations), 0) // rows
    repeat = (repeat == lax.broadcasted_iota(jnp.int32, (total, destinations), 1)).astype(f32)
    table_copy.wait()
    chosen = dot_last(repeat, table[...].astype(f32))
    offset = chosen - (lax.axis_index("seq") * local_blocks).astype(f32)
    slot = lax.broadcasted_iota(jnp.int32, (total, slots), 1)
    inside = (chosen >= 0) & (offset >= 0) & (offset < local_blocks) & (slot > 0)
    which = jnp.sum(jnp.where(inside, offset, 0.0), axis=1, keepdims=True)
    width = local_blocks * rows
    row = lax.broadcasted_iota(jnp.int32, (total, width), 0) % rows
    column = lax.broadcasted_iota(jnp.int32, (total, width), 1)
    pick = (column.astype(f32) == which * rows + row.astype(f32)).astype(bf16)

    for copy in copies:
        copy.wait()
    rope_rows = turned[...].astype(f32)
    rope[...] = jnp.concatenate([rope_rows, rope_rows], axis=0).T.astype(bf16)
    parts = []
    for k in range(local_blocks):
        parts.append(
            jnp.concatenate(
                [
                    jnp.where(is_low, wide[k, :, 0:half_width], wide[k, :, half_width:]),
                    jnp.where(is_low, narrow[k], rope[spots[k], :]),
                ],
                axis=1,
            )
        )
    own_rope[...] = rope[(local_blocks - 1) * block :, :]
    share = jnp.concatenate(parts, axis=0)
    packed[...] = dot(pick, share).astype(bf16)


def place(side):
    head = lax.axis_index("head")
    core = lax.rem(lax.axis_index("seq"), 2)
    x, y = lax.div(head, side), lax.rem(head, side)
    return core, jnp.where(core == 0, y, x), jnp.where(core == 0, x, y)


def head_at(side, core, u, v):
    return jnp.where(core == 0, v * side + u, u * side + v)


def query_kernel(
    side, groups, sel_turned, latent, rope, index, weight, out0, out1, out2, out3, bias, key_bias
):
    outs = (out0, out1, out2, out3)
    chunks = side * side
    slots, destinations = sel_turned.shape
    query_rows = latent.shape[0] // chunks
    lanes = out0.shape[2]
    index_rows = index.shape[0] // chunks
    rope_rows = rope.shape[0] // chunks
    weight_rows = weight.shape[0] // chunks
    tall = index_rows + weight_rows
    rest = query_rows - tall
    core, u, _ = place(side)
    for k in range(side):
        out = outs[k]
        for v in range(side):
            chunk = head_at(side, core, lax.rem(u + k, side), v)

            def at(count, size, begin=0):
                return pl.ds(pl.multiple_of(chunk * count + begin, 16), size)

            out[v, 0:query_rows, :] = latent[at(query_rows, query_rows), 0:lanes]
            out[v, query_rows : query_rows + tall, 0:128] = latent[at(query_rows, tall), lanes:]
            out[v, query_rows : query_rows + rest, 128:256] = latent[
                at(query_rows, rest, tall), lanes:
            ]
            out[v, query_rows + rest : query_rows + tall, 128:256] = rope[
                at(rope_rows, rope_rows), :
            ]
            out[v, query_rows : query_rows + index_rows, 256:384] = index[
                at(index_rows, index_rows), :
            ]
            out[v, query_rows + index_rows : query_rows + tall, 256:384] = weight[
                at(weight_rows, weight_rows), :
            ]
    tokens, total = bias.shape
    rows = total // slots // groups
    share_rows = (slots - 1) * rows
    remote = groups * share_rows
    here = lax.axis_index("seq")
    head = lax.axis_index("head")
    table = sel_turned[...].astype(f32)
    pick = lax.broadcasted_iota(jnp.int32, (tokens, destinations), 1) == here
    valid = (dot_last(pick.astype(f32), table) >= 0).astype(f32)
    key = lax.broadcasted_iota(jnp.int32, (slots, total), 1)
    slot = lax.div(lax.rem(key, share_rows), rows) + 1
    mark = (slot == lax.broadcasted_iota(jnp.int32, (slots, total), 0)).astype(f32)
    key = lax.broadcasted_iota(jnp.int32, (tokens, total), 1)
    token = lax.broadcasted_iota(jnp.int32, (tokens, total), 0) + head * tokens
    good = ((key < remote) & (dot(valid, mark) > 0)) | ((key >= remote) & (key - remote <= token))
    masks = jnp.where(good, 0.0, -1e30)
    bias[...] = masks
    tall_masks = jnp.concatenate([masks, jnp.zeros((128 - tokens, total), f32)], axis=0)
    key_bias[...] = tall_masks.T.astype(bf16)


def stage_kernel(local_blocks, sel, fetched, in0, in1, in2, in3, outgoing):
    parts = (in0, in1, in2, in3)
    slots = sel.shape[0]
    rows = fetched.shape[1]
    height = in0.shape[1]
    here = lax.axis_index("seq")
    first = (slots - 1) * rows
    for j in range(1, slots):
        piece = fetched[lax.div(jnp.maximum(sel[j, here], 0), local_blocks)]
        for v in range(len(parts)):
            outgoing[v, (j - 1) * rows : j * rows, :] = piece
    for k in range(len(parts)):
        for v in range(len(parts)):
            at = first + k * height
            outgoing[v, at : at + height, :] = parts[k][v]


def spread_kernel(staged, outgoing):
    side, height, _ = outgoing.shape
    share = height // side
    for v in range(side):
        piece = staged[v, 0:share, :]
        for u in range(side):
            outgoing[u, v * share : (v + 1) * share, :] = piece


def compute_kernel(
    loss_weight,
    index_scale,
    index_heads,
    staged,
    spread_shares,
    bias,
    key_bias,
    own_rope,
    latent,
    index,
    grad_queries,
    grad_weights,
    shares,
    keys,
    index_k,
    scores,
    highest,
    active,
    slope,
    grad_pre,
    logit_rows,
    target_rows,
    grad_keys,
    sems,
):
    sources, share_rows, lanes = spread_shares.shape
    step = staged.shape[0]
    groups = sources // 2
    tokens, total = bias.shape
    block = own_rope.shape[0]
    latent_width = latent.shape[1]
    half_width = latent_width // 2
    index_width = index.shape[1]
    query_rows = target_rows.shape[0]
    heads = query_rows // tokens
    index_rows = logit_rows.shape[0]
    remote = groups * share_rows
    tile = 2 * 128
    tiles = total // tile
    score_rows = step * query_rows
    chunk = step * index_rows
    height = (staged.shape[1] - share_rows) // step
    tall = height - query_rows
    rest = query_rows - tall
    core, own_u, _ = place(step)
    own_rows = pl.ds(latent.shape[0] - block, block)
    copies = (
        pltpu.make_async_copy(
            latent.at[own_rows], keys.at[pl.ds(remote, block), pl.ds(0, latent_width)], sems.at[0]
        ),
        pltpu.make_async_copy(index.at[own_rows], index_k.at[pl.ds(remote, block)], sems.at[1]),
    )
    for copy in copies:
        copy.start()

    for g in range(groups):
        at = slice(g * share_rows, (g + 1) * share_rows)
        x, y = g // step, g % step
        low = jnp.where(core == 0, y * step + x, x * step + y)
        x = x + step // 2
        high = jnp.where(core == 0, y * step + x, x * step + y)
        keys[at, 0:half_width] = spread_shares[low, :, 0:half_width]
        index_k[at, :] = spread_shares[low, :, half_width:]
        keys[at, half_width : latent_width + 128] = spread_shares[high]
    keys[remote:total, latent_width : latent_width + 128] = own_rope[...]
    keys[:, latent_width + 128 :] = key_bias[...]
    target_rows[...] = jnp.zeros_like(target_rows)
    logit_rows[...] = jnp.zeros_like(logit_rows)
    for copy in copies:
        copy.wait()

    lane_low = lax.broadcasted_iota(jnp.int32, (query_rows // 2, 128), 1) < 64
    lane_low = lane_low.astype(f32)
    keep_low = lane_low.astype(bf16)
    keep_high = (1.0 - lane_low).astype(bf16)

    on_token = (
        lax.broadcasted_iota(jnp.int32, (query_rows, 128), 0) // heads
        == lax.broadcasted_iota(jnp.int32, (query_rows, 128), 1)
    ).astype(bf16)

    def queries_of(v):
        pieces = []
        for k in range(step):
            at = share_rows + k * height
            below = at + query_rows
            rope = staged[v, below + rest : below + tall, 128:256]
            pieces.append(
                jnp.concatenate(
                    [
                        staged[v, at:below, :],
                        jnp.concatenate(
                            [
                                staged[v, below : below + tall, 0:128],
                                staged[v, below : below + rest, 128:256],
                            ],
                            axis=0,
                        ),
                        jnp.concatenate([rope * keep_low, rope * keep_high], axis=0),
                        on_token,
                    ],
                    axis=1,
                )
            )
        return jnp.concatenate(pieces, axis=0)

    def index_queries_of(v):
        pieces = []
        for k in range(step):
            below = share_rows + k * height + query_rows
            pieces.append(staged[v, below : below + index_rows, 256:384])
        return jnp.concatenate(pieces, axis=0)

    def weights_of(v):
        columns = []
        for k in range(step):
            below = share_rows + k * height + query_rows
            pieces = staged[v, below + index_rows : below + tall, 256:384].astype(f32)
            early = lax.broadcasted_iota(jnp.int32, pieces.shape, 1) < 3
            columns.append(jnp.sum(jnp.where(early, pieces, 0.0), axis=1, keepdims=True))
            columns.append(jnp.sum(jnp.where(early, 0.0, pieces), axis=1, keepdims=True))
        return jnp.concatenate(columns, axis=0).reshape(step, index_rows, 1)

    def source_of(v, k):
        return head_at(step, core, lax.rem(own_u + step - k, step), v)

    tile_at = [slice(k * tile, (k + 1) * tile) for k in range(tiles)]

    def soften(c, state, k):
        score_at = slice(c * score_rows, (c + 1) * score_rows)
        if k == 0:
            state["top"] = jnp.max(state["best"], axis=1, keepdims=True)
            state["sums"] = jnp.zeros((score_rows, 128), f32)
        if k == tiles // 2:
            weight = 1.0 / ((heads * sources) * jnp.sum(state["sums"], axis=1, keepdims=True))
            state["weight"] = weight.reshape(step, query_rows, 1)
        for i in range(2):
            if k < tiles // 2:
                at = tile_at[2 * k + i]
                power = jnp.exp((scores[score_at, at] - state["top"]) * score_scale)
                scores[score_at, at] = power
                state["sums"] = state["sums"] + (power[:, 0:128] + power[:, 128:256])
            else:
                at = tile_at[2 * k - tiles + i]
                power = scores[score_at, at].reshape(step, query_rows, tile)
                target_rows[:, at] += jnp.sum(power * state["weight"], axis=0)

    state = None
    for c in range(sources // step):
        score_at = slice(c * score_rows, (c + 1) * score_rows)
        rows = slice(c * chunk, (c + 1) * chunk)
        queries = queries_of(c)
        index_q = index_queries_of(c)
        weights = weights_of(c)
        best = jnp.full((score_rows, 128), -3e38, f32)
        for k in range(tiles):
            at = tile_at[k]
            part = dot_last(queries, keys[at, :])
            scores[score_at, at] = part
            best = jnp.maximum(best, jnp.maximum(part[:, 0:128], part[:, 128:256]))
            act, rate = gelu_pair(dot_last(index_q, index_k[at, :]) * index_scale)
            active[rows, at] = act
            slope[rows, at] = rate
            logit_rows[:, at] += jnp.sum(
                act.reshape(step, index_rows, tile) * weights, axis=0
            )
            if state is not None:
                soften(c - 1, state, k)
        state = {"best": best}
    for k in range(tiles):
        soften(sources // step - 1, state, k)

    def gather(count):
        return (
            lax.broadcasted_iota(jnp.int32, (tokens, tokens * count), 1) // count
            == lax.broadcasted_iota(jnp.int32, (tokens, tokens * count), 0)
        ).astype(f32)

    spread = (
        lax.broadcasted_iota(jnp.int32, (index_rows, tokens), 0) // index_heads
        == lax.broadcasted_iota(jnp.int32, (index_rows, tokens), 1)
    ).astype(bf16)
    logits = dot(gather(index_heads), logit_rows[...], lax.Precision.HIGHEST) + bias[...]
    target = dot(gather(heads), target_rows[...], lax.Precision.HIGHEST)
    likely = jnp.exp(logits - jnp.max(logits, axis=1, keepdims=True))
    predicted = likely / jnp.sum(likely, axis=1, keepdims=True)
    grad_logits = jnp.where(
        bias[...] == 0.0, loss_weight * (predicted - target), 0.0
    ).astype(bf16)
    logit_rows[...] = dot(spread, grad_logits)

    for c in range(sources // step):
        rows = slice(c * chunk, (c + 1) * chunk)
        weights = weights_of(c) * index_scale
        sums = jnp.zeros((chunk, 128), f32)
        for k in range(tiles):
            at = slice(k * tile, (k + 1) * tile)
            grad = logit_rows[:, at][None]
            product = (
                active[rows, at].reshape(step, index_rows, tile) * grad
            ).reshape(chunk, tile)
            sums = sums + (product[:, 0:128] + product[:, 128:256])
            grad_pre[rows, at] = (
                (slope[rows, at].reshape(step, index_rows, tile) * (grad * weights))
                .reshape(chunk, tile)
                .astype(bf16)
            )
        turned = jnp.broadcast_to(jnp.sum(sums, axis=1, keepdims=True), (chunk, 128)).T
        for k in range(step):
            own = turned[0:8] if k == 0 else pltpu.roll(turned[0:8], 128 - k * index_rows, 1)
            own_high = own.astype(bf16)
            own_low = (own - own_high.astype(f32)).astype(bf16)
            grad_weights[source_of(c, k)] = jnp.concatenate([own_high, own_low], axis=0)

    result = dot(grad_pre[...], index_k[...]).astype(bf16)
    for v in range(step):
        for k in range(step):
            at = (v * step + k) * index_rows
            grad_queries[source_of(v, k)] = result[at : at + index_rows]
    turned = jnp.concatenate([index_queries_of(v) for v in range(step)], axis=0)
    turned = turned.astype(f32).T.astype(bf16)
    for k in range(tiles):
        at = slice(k * tile, (k + 1) * tile)
        grad_keys[at, :] = dot(turned, grad_pre[:, at]).T
    small = block // sources
    slots = total // block
    for g in range(groups):
        own = grad_keys[remote + g * 2 * small : remote + (g + 1) * 2 * small, :]
        own = own.reshape(1, 2, small, index_width)
        rest_keys = grad_keys[g * share_rows : (g + 1) * share_rows, :]
        rest_keys = rest_keys.reshape(slots - 1, 2, small, index_width)
        both_keys = jnp.concatenate([own, rest_keys], axis=0)
        for i in range(2):
            shares[i * groups + g] = both_keys[:, i].reshape(block, index_width).astype(bf16)


def last_kernel(groups, index_heads, final, grad_queries, grad_weights, grad_keys):
    sources, _, width = final.shape
    block = grad_weights.shape[1]
    tokens = block // sources
    index_rows = tokens * index_heads
    local_blocks = grad_keys.shape[0] // block
    small = block // sources
    own_rows = local_blocks * small
    second = own_rows + index_rows
    for k in range(sources):
        part = final[k, 0:own_rows, :].astype(f32)
        half, group = k // groups, k % groups
        for j in range(local_blocks):
            at = j * block + group * 2 * small + half * small
            grad_keys[at : at + small, :] = part[j * small : (j + 1) * small]
        grad_queries[k * index_rows : (k + 1) * index_rows, :] = final[
            k, own_rows:second, :
        ].astype(f32)
    row = lax.broadcasted_iota(jnp.int32, (block, width), 0)
    lane = lax.broadcasted_iota(jnp.int32, (block, width), 1)
    keep = (lane < index_rows) & (lax.div(lane, index_heads) == row % tokens)
    which = lax.broadcasted_iota(jnp.int32, (8, width), 0)
    head = lax.rem(lax.broadcasted_iota(jnp.int32, (8, width), 1), index_heads)
    fold = (which == head).astype(bf16)
    result = jnp.zeros((8, block), f32)
    for i in range(2):
        lines = []
        for k in range(sources):
            whole = final[k, second : second + 16, :].astype(f32)
            lines.append(jnp.broadcast_to(whole[8 * i : 8 * i + 1], (tokens, width)))
        lines = jnp.concatenate(lines, axis=0)
        result = result + dot_last(fold, jnp.where(keep, lines, 0.0).astype(bf16))
    grad_weights[...] = result[0:index_heads]


def exchange(array, axis, groups=None):
    return lax.all_to_all(
        array, axis, split_axis=0, concat_axis=0, tiled=True, axis_index_groups=groups
    )


def exchange_alone(array, axis, others, groups=None):
    array, others = lax.optimization_barrier((array, others))
    return lax.optimization_barrier((exchange(array, axis, groups), others))


def flat_index(side, seq_count, u, v, seq):
    x, y = (v, u) if seq % 2 == 0 else (u, v)
    return (x * side + y) * seq_count + seq


def lines(side, seq_count, along_u):
    return [
        [
            flat_index(side, seq_count, *((i, j) if along_u else (j, i)), seq)
            for i in range(side)
        ]
        for seq in range(seq_count)
        for j in range(side)
    ]


def shift_along_u(side, seq_count, k):
    return [
        (
            flat_index(side, seq_count, u, v, seq),
            flat_index(side, seq_count, (u + k) % side, v, seq),
        )
        for seq in range(seq_count)
        for u in range(side)
        for v in range(side)
    ]


def pad_lanes(array, width):
    return jnp.pad(array, [(0, 0)] * (array.ndim - 1) + [(0, width - array.shape[-1])])


def body(
    q_latent, q_rope, latent_cache, rope_keys, index_queries, index_weights, index_keys, sel_blocks
):
    head_count = lax.axis_size("head")
    seq_count = lax.axis_size("seq")
    head_index = lax.axis_index("head")
    seq_index = lax.axis_index("seq")
    block, heads, latent_width = q_latent.shape
    rope_width = q_rope.shape[2]
    index_heads, index_width = index_queries.shape[1:]
    slot_count = sel_blocks.shape[1]
    local_blocks = latent_cache.shape[0] // block
    index_scale = index_width ** (-0.5)
    loss_weight = float(slot_count * block)
    groups = head_count // 2
    side = math.isqrt(head_count)
    rows = block // groups
    small = rows // 2
    tokens = block // head_count
    half_width = latent_width // 2
    lanes = half_width + index_width
    remote_slots = slot_count - 1

    later = sel_blocks[:, 1:]
    offsets = later - seq_index * local_blocks
    inside = (later >= 0) & (offsets >= 0) & (offsets < local_blocks)
    wanted = jnp.any(inside, axis=1)
    which = jnp.sum(jnp.where(inside, offsets, 0), axis=1)
    sel_row = lax.dynamic_index_in_dim(sel_blocks, seq_index, 0, keepdims=False)
    slot_valid = sel_row >= 0
    source = jnp.where(slot_valid, sel_row // local_blocks, 0)
    in_vmem = pl.BlockSpec(memory_space=pltpu.VMEM)
    in_smem = pl.BlockSpec(memory_space=pltpu.SMEM)
    in_place = pl.BlockSpec(memory_space=pl.ANY)

    packed, own_rope = pl.pallas_call(
        functools.partial(first_kernel, groups),
        out_shape=(
            jax.ShapeDtypeStruct((seq_count * rows, lanes), bf16),
            jax.ShapeDtypeStruct((block, 2 * rope_width), bf16),
        ),
        in_specs=[in_place] * 4,
        out_specs=(in_vmem, in_vmem),
        scratch_shapes=[
            pltpu.VMEM((local_blocks, rows, latent_width), bf16),
            pltpu.VMEM((local_blocks, rows, index_width), bf16),
            pltpu.VMEM((rope_width, local_blocks * block), bf16),
            pltpu.VMEM((local_blocks * block, 2 * rope_width), bf16),
            pltpu.VMEM((slot_count, seq_count), jnp.int32),
            pltpu.SemaphoreType.DMA((2 + 2 * local_blocks,)),
        ],
        compiler_params=pltpu.CompilerParams(vmem_limit_bytes=60 * 1024 * 1024),
    )(sel_blocks.T, latent_cache, rope_keys.T, index_keys)
    fetched = exchange(packed.reshape(seq_count, rows, lanes), "seq")

    share_rows = remote_slots * rows
    query_rows = tokens * heads
    index_rows = tokens * index_heads
    latent_parts = q_latent.reshape(block * heads, latent_width)
    rope_parts = q_rope.reshape(head_count, 2, query_rows // 2, rope_width)
    rope_parts = jnp.concatenate([rope_parts[:, 0], rope_parts[:, 1]], axis=-1)
    rope_parts = rope_parts.reshape(head_count * query_rows // 2, 2 * rope_width)
    index_parts = index_queries.reshape(head_count * index_rows, index_width)
    weight_parts = index_weights.reshape(head_count, 2, index_rows // 2, 1)
    high = lax.reduce_precision(weight_parts, 8, 7)
    middle = lax.reduce_precision(weight_parts - high, 8, 7)
    low = weight_parts - high - middle
    pieces = jnp.concatenate([high, middle, low], axis=-1).astype(bf16)
    pieces = pad_lanes(jnp.concatenate([pieces[:, 0], pieces[:, 1]], axis=-1), 128)
    pieces = pieces.reshape(head_count * index_rows // 2, 128)
    height = query_rows + index_rows + index_rows // 2
    total = slot_count * block
    axes = ("head", "seq")
    *parts, bias, key_bias = pl.pallas_call(
        functools.partial(query_kernel, side, groups),
        out_shape=tuple([jax.ShapeDtypeStruct((side, height, lanes), bf16)] * side)
        + (
            jax.ShapeDtypeStruct((tokens, total), f32),
            jax.ShapeDtypeStruct((total, 128), bf16),
        ),
        in_specs=[in_vmem] * 5,
        out_specs=tuple([in_vmem] * (side + 2)),
        compiler_params=pltpu.CompilerParams(vmem_limit_bytes=24 * 1024 * 1024),
    )(sel_blocks.T, latent_parts, rope_parts, index_parts, pieces)
    for k in range(1, side):
        parts[k] = lax.ppermute(parts[k], axes, shift_along_u(side, seq_count, k))
    outgoing = pl.pallas_call(
        functools.partial(stage_kernel, local_blocks),
        out_shape=jax.ShapeDtypeStruct((side, share_rows + side * height, lanes), bf16),
        in_specs=[in_smem] + [in_vmem] * (side + 1),
        out_specs=in_vmem,
        compiler_params=pltpu.CompilerParams(vmem_limit_bytes=24 * 1024 * 1024),
    )(sel_blocks.T, fetched, *parts)
    found = (source[1:][None, :] == jnp.arange(seq_count)[:, None]) & slot_valid[1:][None, :]
    slot_of = jnp.sum(jnp.where(found, jnp.arange(1, slot_count)[None, :], 0), axis=1)
    owner = wanted[:, None] & (which[:, None] == jnp.arange(local_blocks)[None, :])
    owner = owner.astype(f32)
    later = (bias, key_bias, own_rope, slot_of, owner)
    staged, later = exchange_alone(outgoing, axes, later, lines(side, seq_count, False))
    spread = pl.pallas_call(
        spread_kernel,
        out_shape=jax.ShapeDtypeStruct((side, side * share_rows, lanes), bf16),
        in_specs=[in_vmem],
        out_specs=in_vmem,
        compiler_params=pltpu.CompilerParams(vmem_limit_bytes=16 * 1024 * 1024),
    )(staged)
    spread, (staged, bias, key_bias, own_rope, slot_of, owner) = exchange_alone(
        spread, axes, (staged, *later), lines(side, seq_count, True)
    )

    all_rows = head_count * index_rows
    grad_queries, grad_weights, shares = pl.pallas_call(
        functools.partial(compute_kernel, loss_weight, index_scale, index_heads),
        out_shape=(
            jax.ShapeDtypeStruct((head_count, index_rows, index_width), bf16),
            jax.ShapeDtypeStruct((head_count, 16, 128), bf16),
            jax.ShapeDtypeStruct((head_count, slot_count * small, index_width), bf16),
        ),
        in_specs=[in_vmem] * 5 + [in_place] * 2,
        out_specs=(in_vmem, in_vmem, in_vmem),
        scratch_shapes=[
            pltpu.VMEM((total, latent_width + 256), bf16),
            pltpu.VMEM((total, index_width), bf16),
            pltpu.VMEM((head_count * query_rows, total), f32),
            pltpu.VMEM((head_count * query_rows, 128), f32),
            pltpu.VMEM((all_rows, total), f32),
            pltpu.VMEM((all_rows, total), f32),
            pltpu.VMEM((all_rows, total), bf16),
            pltpu.VMEM((index_rows, total), f32),
            pltpu.VMEM((query_rows, total), f32),
            pltpu.VMEM((total, index_width), f32),
            pltpu.SemaphoreType.DMA((2,)),
        ],
        compiler_params=pltpu.CompilerParams(vmem_limit_bytes=36 * 1024 * 1024),
    )(
        staged,
        spread.reshape(head_count, share_rows, lanes),
        bias,
        key_bias,
        own_rope,
        latent_cache,
        index_keys,
    )

    collected, (grad_queries, grad_weights, slot_of, owner) = exchange_alone(
        shares, "head", (grad_queries, grad_weights, slot_of, owner)
    )
    summed = jnp.sum(collected.astype(f32), axis=0).reshape(slot_count, small, index_width)
    own_sum = summed[0]
    returned, (own_sum, grad_queries, grad_weights, owner) = exchange_alone(
        jnp.take(summed, slot_of, axis=0).astype(bf16),
        "seq",
        (own_sum, grad_queries, grad_weights, owner),
    )
    owned = jnp.sum(owner[:, :, None, None] * returned.astype(f32)[:, None], axis=0)
    owned = owned.at[local_blocks - 1].add(own_sum)

    own_rows = local_blocks * small
    last = jnp.concatenate(
        [
            jnp.broadcast_to(
                owned.reshape(own_rows, index_width).astype(bf16), (head_count, own_rows, index_width)
            ),
            grad_queries,
            grad_weights,
        ],
        axis=1,
    )
    final, _ = exchange_alone(last, "head", ())
    out_queries, out_weights, grad_keys = pl.pallas_call(
        functools.partial(last_kernel, groups, index_heads),
        out_shape=(
            jax.ShapeDtypeStruct((block * index_heads, index_width), f32),
            jax.ShapeDtypeStruct((index_heads, block), f32),
            jax.ShapeDtypeStruct((local_blocks * block, index_width), f32),
        ),
        in_specs=[in_vmem],
        out_specs=(in_vmem, in_vmem, in_vmem),
        compiler_params=pltpu.CompilerParams(vmem_limit_bytes=16 * 1024 * 1024),
    )(final)
    return (out_queries.reshape(block, index_heads, index_width), out_weights.T, grad_keys)


def solution(mesh):
    placed = (
        P("seq", "head", None),
        P("seq", "head", None),
        P("seq", None),
        P("seq", None),
        P("seq", "head", None),
        P("seq", "head"),
        P("seq", None),
        P(),
    )
    return jax.shard_map(
        body,
        mesh=mesh,
        in_specs=placed,
        out_specs=(P("seq", "head", None), P("seq", "head"), P("seq", None)),
        check_vma=False,
    )
```

```python
import functools
import math

import jax
import jax.numpy as jnp
from jax import lax
from jax.experimental import pallas as pl
from jax.experimental.pallas import tpu as pltpu
from jax.sharding import PartitionSpec as P

score_scale = 192.0 ** (-0.5)
gelu_coef = math.sqrt(2.0 / math.pi)
cubic_coef = 0.044715
bf16 = jnp.bfloat16
f32 = jnp.float32


def dot_last(a, b):
    return lax.dot_general(a, b, (((1,), (1,)), ((), ())), preferred_element_type=f32)


def dot(a, b, precision=None):
    return jnp.dot(a, b, preferred_element_type=f32, precision=precision)


def gelu_pair(values):
    square = values * values
    tangent = jnp.tanh(values * (gelu_coef + (gelu_coef * cubic_coef) * square))
    upper = 0.5 + 0.5 * tangent
    active = values * upper
    slope = upper + active * (1.0 - upper) * (
        2.0 * gelu_coef + (6.0 * gelu_coef * cubic_coef) * square
    )
    return (active, slope)


def first_kernel(
    groups,
    sel_turned,
    latent,
    rope_turned,
    index,
    packed,
    own_rope,
    wide,
    narrow,
    turned,
    rope,
    table,
    sems,
):
    slots, destinations = sel_turned.shape
    variants, local_blocks, rows, latent_width = wide.shape
    block = latent.shape[0] // local_blocks
    half_width = latent_width // 2
    side = groups // 2
    head = lax.axis_index("head")
    x, y = lax.div(head, side), lax.rem(head, side)
    spots = []
    lows = []
    count = variants * local_blocks
    copies = [pltpu.make_async_copy(rope_turned, turned, sems.at[0])]
    table_copy = pltpu.make_async_copy(sel_turned, table, sems.at[1])
    table_copy.start()
    for i, (u, v) in enumerate(((y, x), (x, y))):
        group = lax.rem(v, 2) * side + u
        lows.append(v < side // 2)
        for k in range(local_blocks):
            at = pl.ds(pl.multiple_of(k * block + group * rows, rows), rows)
            n = i * local_blocks + k
            spots.append(at)
            copies.append(pltpu.make_async_copy(latent.at[at], wide.at[i, k], sems.at[2 + n]))
            copies.append(
                pltpu.make_async_copy(index.at[at], narrow.at[i, k], sems.at[2 + count + n])
            )
    for copy in copies:
        copy.start()

    total = packed.shape[0]
    repeat = lax.broadcasted_iota(jnp.int32, (total, destinations), 0) // rows
    repeat = (repeat == lax.broadcasted_iota(jnp.int32, (total, destinations), 1)).astype(f32)
    table_copy.wait()
    chosen = dot_last(repeat, table[...].astype(f32))
    offset = chosen - (lax.axis_index("seq") * local_blocks).astype(f32)
    slot = lax.broadcasted_iota(jnp.int32, (total, slots), 1)
    inside = (chosen >= 0) & (offset >= 0) & (offset < local_blocks) & (slot > 0)
    which = jnp.sum(jnp.where(inside, offset, 0.0), axis=1, keepdims=True)
    width = variants * local_blocks * rows
    row = lax.broadcasted_iota(jnp.int32, (total, width), 0)
    start = (row // rows) % variants * (local_blocks * rows) + row % rows
    column = lax.broadcasted_iota(jnp.int32, (total, width), 1)
    pick = (column.astype(f32) == which * rows + start.astype(f32)).astype(bf16)

    for copy in copies:
        copy.wait()
    rope_rows = turned[...].astype(f32)
    rope[...] = jnp.concatenate([rope_rows, rope_rows], axis=0).T.astype(bf16)
    parts = []
    for i in range(variants):
        for k in range(local_blocks):
            parts.append(
                jnp.concatenate(
                    [
                        jnp.where(lows[i], wide[i, k, :, 0:half_width], wide[i, k, :, half_width:]),
                        jnp.where(lows[i], narrow[i, k], rope[spots[i * local_blocks + k], :]),
                    ],
                    axis=1,
                )
            )
    own_rope[...] = rope[(local_blocks - 1) * block :, :]
    share = jnp.concatenate(parts, axis=0)
    packed[...] = dot(pick, share).astype(bf16)


def place(side):
    head = lax.axis_index("head")
    core = lax.rem(lax.axis_index("seq"), 2)
    x, y = lax.div(head, side), lax.rem(head, side)
    return core, jnp.where(core == 0, y, x), jnp.where(core == 0, x, y)


def head_at(side, core, u, v):
    return jnp.where(core == 0, v * side + u, u * side + v)


def query_kernel(
    side, groups, sel_turned, latent, rope, index, weight, out0, out1, out2, out3, bias, key_bias
):
    outs = (out0, out1, out2, out3)
    chunks = side * side
    slots, destinations = sel_turned.shape
    query_rows = latent.shape[0] // chunks
    lanes = out0.shape[2]
    index_rows = index.shape[0] // chunks
    rope_rows = rope.shape[0] // chunks
    weight_rows = weight.shape[0] // chunks
    tall = index_rows + weight_rows
    rest = query_rows - tall
    core, u, _ = place(side)
    for k in range(side):
        out = outs[k]
        for v in range(side):
            chunk = head_at(side, core, lax.rem(u + k, side), v)

            def at(count, size, begin=0):
                return pl.ds(pl.multiple_of(chunk * count + begin, 16), size)

            out[v, 0:query_rows, :] = latent[at(query_rows, query_rows), 0:lanes]
            out[v, query_rows : query_rows + tall, 0:128] = latent[at(query_rows, tall), lanes:]
            out[v, query_rows : query_rows + rest, 128:256] = latent[
                at(query_rows, rest, tall), lanes:
            ]
            out[v, query_rows + rest : query_rows + tall, 128:256] = rope[
                at(rope_rows, rope_rows), :
            ]
            out[v, query_rows : query_rows + index_rows, 256:384] = index[
                at(index_rows, index_rows), :
            ]
            out[v, query_rows + index_rows : query_rows + tall, 256:384] = weight[
                at(weight_rows, weight_rows), :
            ]
    tokens, total = bias.shape
    rows = total // slots // groups
    share_rows = (slots - 1) * rows
    remote = groups * share_rows
    here = lax.axis_index("seq")
    head = lax.axis_index("head")
    table = sel_turned[...].astype(f32)
    pick = lax.broadcasted_iota(jnp.int32, (tokens, destinations), 1) == here
    valid = (dot_last(pick.astype(f32), table) >= 0).astype(f32)
    key = lax.broadcasted_iota(jnp.int32, (slots, total), 1)
    slot = lax.div(lax.rem(key, share_rows), rows) + 1
    mark = (slot == lax.broadcasted_iota(jnp.int32, (slots, total), 0)).astype(f32)
    key = lax.broadcasted_iota(jnp.int32, (tokens, total), 1)
    token = lax.broadcasted_iota(jnp.int32, (tokens, total), 0) + head * tokens
    good = ((key < remote) & (dot(valid, mark) > 0)) | ((key >= remote) & (key - remote <= token))
    masks = jnp.where(good, 0.0, -1e30)
    bias[...] = masks
    tall_masks = jnp.concatenate([masks, jnp.zeros((128 - tokens, total), f32)], axis=0)
    key_bias[...] = tall_masks.T.astype(bf16)


def stage_kernel(local_blocks, sel, fetched, in0, in1, in2, in3, outgoing):
    parts = (in0, in1, in2, in3)
    slots = sel.shape[0]
    rows = fetched.shape[1]
    height = in0.shape[1]
    here = lax.axis_index("seq")
    first = (slots - 1) * rows
    for j in range(1, slots):
        piece = fetched[lax.div(jnp.maximum(sel[j, here], 0), local_blocks)]
        for v in range(len(parts)):
            outgoing[v, (j - 1) * rows : j * rows, :] = piece
    for k in range(len(parts)):
        for v in range(len(parts)):
            at = first + k * height
            outgoing[v, at : at + height, :] = parts[k][v]


def spread_kernel(share, staged, outgoing):
    side = outgoing.shape[0]
    lane_low = (lax.broadcasted_iota(jnp.int32, (share, 128), 1) < 64).astype(f32)
    third, fourth = staged[2, 0:share, :], staged[3, 0:share, :]
    rope = third[:, 256:384] * lane_low.astype(bf16) + fourth[:, 256:384] * (
        1.0 - lane_low
    ).astype(bf16)
    long = share * 2 // 3
    rest = share - long
    for u in range(side):
        outgoing[u, 0:share, :] = staged[0, 0:share, :]
        outgoing[u, share : 2 * share, :] = staged[1, 0:share, :]
        outgoing[u, 2 * share : 3 * share, 0:256] = third[:, 0:256]
        outgoing[u, 2 * share : 3 * share, 256:384] = rope
        at = 3 * share
        outgoing[u, at : at + long, 0:256] = fourth[0:long, 0:256]
        outgoing[u, at : at + rest, 256:384] = fourth[long:, 0:128]
        outgoing[u, at + rest : at + long, 256:384] = fourth[long:, 128:256]


def compute_kernel(
    loss_weight,
    index_scale,
    index_heads,
    staged,
    spread_shares,
    bias,
    key_bias,
    own_rope,
    latent,
    index,
    grad_queries,
    grad_weights,
    shares,
    keys,
    index_k,
    scores,
    highest,
    active,
    slope,
    grad_pre,
    logit_rows,
    target_rows,
    grad_keys,
    sems,
):
    step = staged.shape[0]
    sources = step * step
    groups = sources // 2
    tokens, total = bias.shape
    block = own_rope.shape[0]
    latent_width = latent.shape[1]
    half_width = latent_width // 2
    index_width = index.shape[1]
    query_rows = target_rows.shape[0]
    heads = query_rows // tokens
    index_rows = logit_rows.shape[0]
    remote = total - block
    share_rows = remote // groups
    tile = 2 * 128
    tiles = total // tile
    score_rows = step * query_rows
    chunk = step * index_rows
    height = (staged.shape[1] - share_rows) // step
    tall = height - query_rows
    rest = query_rows - tall
    core, own_u, _ = place(step)
    own_rows = pl.ds(latent.shape[0] - block, block)
    copies = (
        pltpu.make_async_copy(
            latent.at[own_rows], keys.at[pl.ds(remote, block), pl.ds(0, latent_width)], sems.at[0]
        ),
        pltpu.make_async_copy(index.at[own_rows], index_k.at[pl.ds(remote, block)], sems.at[1]),
    )
    for copy in copies:
        copy.start()

    long = share_rows * 2 // 3
    short = share_rows - long
    last = 3 * share_rows
    under = lax.broadcasted_iota(jnp.int32, (share_rows, 128), 1) < 64
    middle_lanes = slice(half_width, latent_width)
    rope_lanes = slice(latent_width, latent_width + 128)
    for u in range(step):
        for i in range(2):
            g = i * step + u
            at = slice(g * share_rows, (g + 1) * share_rows)
            low = slice(i * share_rows, (i + 1) * share_rows)
            keys[at, 0:half_width] = spread_shares[u, low, 0:half_width]
            index_k[at, :] = spread_shares[u, low, half_width:]
        one = slice(u * share_rows, (u + 1) * share_rows)
        two = slice((step + u) * share_rows, (step + u + 1) * share_rows)
        keys[one, middle_lanes] = spread_shares[u, 2 * share_rows : last, 0:half_width]
        top = slice((step + u) * share_rows, (step + u) * share_rows + long)
        low = slice((step + u) * share_rows + long, (step + u + 1) * share_rows)
        keys[top, middle_lanes] = spread_shares[u, last : last + long, 0:half_width]
        keys[low, middle_lanes] = jnp.concatenate(
            [
                spread_shares[u, last : last + short, half_width:],
                spread_shares[u, last + short : last + long, half_width:],
            ],
            axis=1,
        )
        rope = spread_shares[u, 2 * share_rows : last, half_width:].astype(f32)
        swapped = pltpu.roll(rope, 64, 1)
        keys[one, rope_lanes] = jnp.where(under, rope, swapped).astype(bf16)
        keys[two, rope_lanes] = jnp.where(under, swapped, rope).astype(bf16)
    keys[remote:total, latent_width : latent_width + 128] = own_rope[...]
    keys[:, latent_width + 128 :] = key_bias[...]
    target_rows[...] = jnp.zeros_like(target_rows)
    logit_rows[...] = jnp.zeros_like(logit_rows)
    for copy in copies:
        copy.wait()

    lane_low = lax.broadcasted_iota(jnp.int32, (query_rows // 2, 128), 1) < 64
    lane_low = lane_low.astype(f32)
    keep_low = lane_low.astype(bf16)
    keep_high = (1.0 - lane_low).astype(bf16)

    on_token = (
        lax.broadcasted_iota(jnp.int32, (query_rows, 128), 0) // heads
        == lax.broadcasted_iota(jnp.int32, (query_rows, 128), 1)
    ).astype(bf16)

    def queries_of(v):
        pieces = []
        for k in range(step):
            at = share_rows + k * height
            below = at + query_rows
            rope = staged[v, below + rest : below + tall, 128:256]
            pieces.append(
                jnp.concatenate(
                    [
                        staged[v, at:below, :],
                        jnp.concatenate(
                            [
                                staged[v, below : below + tall, 0:128],
                                staged[v, below : below + rest, 128:256],
                            ],
                            axis=0,
                        ),
                        jnp.concatenate([rope * keep_low, rope * keep_high], axis=0),
                        on_token,
                    ],
                    axis=1,
                )
            )
        return jnp.concatenate(pieces, axis=0)

    def index_queries_of(v):
        pieces = []
        for k in range(step):
            below = share_rows + k * height + query_rows
            pieces.append(staged[v, below : below + index_rows, 256:384])
        return jnp.concatenate(pieces, axis=0)

    def weights_of(v):
        columns = []
        for k in range(step):
            below = share_rows + k * height + query_rows
            pieces = staged[v, below + index_rows : below + tall, 256:384].astype(f32)
            early = lax.broadcasted_iota(jnp.int32, pieces.shape, 1) < 3
            columns.append(jnp.sum(jnp.where(early, pieces, 0.0), axis=1, keepdims=True))
            columns.append(jnp.sum(jnp.where(early, 0.0, pieces), axis=1, keepdims=True))
        return jnp.concatenate(columns, axis=0).reshape(step, index_rows, 1)

    def source_of(v, k):
        return head_at(step, core, lax.rem(own_u + step - k, step), v)

    tile_at = [slice(k * tile, (k + 1) * tile) for k in range(tiles)]

    def soften(c, state, k):
        score_at = slice(c * score_rows, (c + 1) * score_rows)
        if k == 0:
            state["top"] = jnp.max(state["best"], axis=1, keepdims=True)
            state["sums"] = jnp.zeros((score_rows, 128), f32)
        if k == tiles // 2:
            weight = 1.0 / ((heads * sources) * jnp.sum(state["sums"], axis=1, keepdims=True))
            state["weight"] = weight.reshape(step, query_rows, 1)
        for i in range(2):
            if k < tiles // 2:
                at = tile_at[2 * k + i]
                power = jnp.exp((scores[score_at, at] - state["top"]) * score_scale)
                scores[score_at, at] = power
                state["sums"] = state["sums"] + (power[:, 0:128] + power[:, 128:256])
            else:
                at = tile_at[2 * k - tiles + i]
                power = scores[score_at, at].reshape(step, query_rows, tile)
                target_rows[:, at] += jnp.sum(power * state["weight"], axis=0)

    state = None
    for c in range(sources // step):
        score_at = slice(c * score_rows, (c + 1) * score_rows)
        rows = slice(c * chunk, (c + 1) * chunk)
        queries = queries_of(c)
        index_q = index_queries_of(c)
        weights = weights_of(c)
        best = jnp.full((score_rows, 128), -3e38, f32)
        for k in range(tiles):
            at = tile_at[k]
            part = dot_last(queries, keys[at, :])
            scores[score_at, at] = part
            best = jnp.maximum(best, jnp.maximum(part[:, 0:128], part[:, 128:256]))
            act, rate = gelu_pair(dot_last(index_q, index_k[at, :]) * index_scale)
            active[rows, at] = act
            slope[rows, at] = rate
            logit_rows[:, at] += jnp.sum(
                act.reshape(step, index_rows, tile) * weights, axis=0
            )
            if state is not None:
                soften(c - 1, state, k)
        state = {"best": best}
    for k in range(tiles):
        soften(sources // step - 1, state, k)

    def gather(count):
        return (
            lax.broadcasted_iota(jnp.int32, (tokens, tokens * count), 1) // count
            == lax.broadcasted_iota(jnp.int32, (tokens, tokens * count), 0)
        ).astype(f32)

    spread = (
        lax.broadcasted_iota(jnp.int32, (index_rows, tokens), 0) // index_heads
        == lax.broadcasted_iota(jnp.int32, (index_rows, tokens), 1)
    ).astype(bf16)
    logits = dot(gather(index_heads), logit_rows[...], lax.Precision.HIGHEST) + bias[...]
    target = dot(gather(heads), target_rows[...], lax.Precision.HIGHEST)
    likely = jnp.exp(logits - jnp.max(logits, axis=1, keepdims=True))
    predicted = likely / jnp.sum(likely, axis=1, keepdims=True)
    grad_logits = jnp.where(
        bias[...] == 0.0, loss_weight * (predicted - target), 0.0
    ).astype(bf16)
    logit_rows[...] = dot(spread, grad_logits)

    for c in range(sources // step):
        rows = slice(c * chunk, (c + 1) * chunk)
        weights = weights_of(c) * index_scale
        sums = jnp.zeros((chunk, 128), f32)
        for k in range(tiles):
            at = slice(k * tile, (k + 1) * tile)
            grad = logit_rows[:, at][None]
            product = (
                active[rows, at].reshape(step, index_rows, tile) * grad
            ).reshape(chunk, tile)
            sums = sums + (product[:, 0:128] + product[:, 128:256])
            grad_pre[rows, at] = (
                (slope[rows, at].reshape(step, index_rows, tile) * (grad * weights))
                .reshape(chunk, tile)
                .astype(bf16)
            )
        turned = jnp.broadcast_to(jnp.sum(sums, axis=1, keepdims=True), (chunk, 128)).T
        for k in range(step):
            own = turned[0:8] if k == 0 else pltpu.roll(turned[0:8], 128 - k * index_rows, 1)
            own_high = own.astype(bf16)
            own_low = (own - own_high.astype(f32)).astype(bf16)
            grad_weights[source_of(c, k)] = jnp.concatenate([own_high, own_low], axis=0)

    result = dot(grad_pre[...], index_k[...]).astype(bf16)
    for v in range(step):
        for k in range(step):
            at = (v * step + k) * index_rows
            grad_queries[source_of(v, k)] = result[at : at + index_rows]
    turned = jnp.concatenate([index_queries_of(v) for v in range(step)], axis=0)
    turned = turned.astype(f32).T.astype(bf16)
    for k in range(tiles):
        at = slice(k * tile, (k + 1) * tile)
        grad_keys[at, :] = dot(turned, grad_pre[:, at]).T
    small = block // sources
    slots = total // block
    for g in range(groups):
        own = grad_keys[remote + g * 2 * small : remote + (g + 1) * 2 * small, :]
        own = own.reshape(1, 2, small, index_width)
        rest_keys = grad_keys[g * share_rows : (g + 1) * share_rows, :]
        rest_keys = rest_keys.reshape(slots - 1, 2, small, index_width)
        both_keys = jnp.concatenate([own, rest_keys], axis=0)
        for i in range(2):
            shares[i * groups + g] = both_keys[:, i].reshape(block, index_width).astype(bf16)


def last_kernel(groups, index_heads, final, grad_queries, grad_weights, grad_keys):
    sources, _, width = final.shape
    block = grad_weights.shape[1]
    tokens = block // sources
    index_rows = tokens * index_heads
    local_blocks = grad_keys.shape[0] // block
    small = block // sources
    own_rows = local_blocks * small
    second = own_rows + index_rows
    for k in range(sources):
        part = final[k, 0:own_rows, :].astype(f32)
        half, group = k // groups, k % groups
        for j in range(local_blocks):
            at = j * block + group * 2 * small + half * small
            grad_keys[at : at + small, :] = part[j * small : (j + 1) * small]
        grad_queries[k * index_rows : (k + 1) * index_rows, :] = final[
            k, own_rows:second, :
        ].astype(f32)
    row = lax.broadcasted_iota(jnp.int32, (block, width), 0)
    lane = lax.broadcasted_iota(jnp.int32, (block, width), 1)
    keep = (lane < index_rows) & (lax.div(lane, index_heads) == row % tokens)
    which = lax.broadcasted_iota(jnp.int32, (8, width), 0)
    head = lax.rem(lax.broadcasted_iota(jnp.int32, (8, width), 1), index_heads)
    fold = (which == head).astype(bf16)
    result = jnp.zeros((8, block), f32)
    for i in range(2):
        lines = []
        for k in range(sources):
            whole = final[k, second : second + 16, :].astype(f32)
            lines.append(jnp.broadcast_to(whole[8 * i : 8 * i + 1], (tokens, width)))
        lines = jnp.concatenate(lines, axis=0)
        result = result + dot_last(fold, jnp.where(keep, lines, 0.0).astype(bf16))
    grad_weights[...] = result[0:index_heads]


def exchange(array, axis, groups=None):
    return lax.all_to_all(
        array, axis, split_axis=0, concat_axis=0, tiled=True, axis_index_groups=groups
    )


def exchange_alone(array, axis, others, groups=None):
    array, others = lax.optimization_barrier((array, others))
    return lax.optimization_barrier((exchange(array, axis, groups), others))


def flat_index(side, seq_count, u, v, seq):
    x, y = (v, u) if seq % 2 == 0 else (u, v)
    return (x * side + y) * seq_count + seq


def lines(side, seq_count, along_u):
    return [
        [
            flat_index(side, seq_count, *((i, j) if along_u else (j, i)), seq)
            for i in range(side)
        ]
        for seq in range(seq_count)
        for j in range(side)
    ]


def shift_along_u(side, seq_count, k):
    return [
        (
            flat_index(side, seq_count, u, v, seq),
            flat_index(side, seq_count, (u + k) % side, v, seq),
        )
        for seq in range(seq_count)
        for u in range(side)
        for v in range(side)
    ]


def pad_lanes(array, width):
    return jnp.pad(array, [(0, 0)] * (array.ndim - 1) + [(0, width - array.shape[-1])])


def body(
    q_latent, q_rope, latent_cache, rope_keys, index_queries, index_weights, index_keys, sel_blocks
):
    head_count = lax.axis_size("head")
    seq_count = lax.axis_size("seq")
    head_index = lax.axis_index("head")
    seq_index = lax.axis_index("seq")
    block, heads, latent_width = q_latent.shape
    rope_width = q_rope.shape[2]
    index_heads, index_width = index_queries.shape[1:]
    slot_count = sel_blocks.shape[1]
    local_blocks = latent_cache.shape[0] // block
    index_scale = index_width ** (-0.5)
    loss_weight = float(slot_count * block)
    groups = head_count // 2
    side = math.isqrt(head_count)
    rows = block // groups
    small = rows // 2
    tokens = block // head_count
    half_width = latent_width // 2
    lanes = half_width + index_width
    remote_slots = slot_count - 1

    later = sel_blocks[:, 1:]
    offsets = later - seq_index * local_blocks
    inside = (later >= 0) & (offsets >= 0) & (offsets < local_blocks)
    wanted = jnp.any(inside, axis=1)
    which = jnp.sum(jnp.where(inside, offsets, 0), axis=1)
    sel_row = lax.dynamic_index_in_dim(sel_blocks, seq_index, 0, keepdims=False)
    slot_valid = sel_row >= 0
    source = jnp.where(slot_valid, sel_row // local_blocks, 0)
    in_vmem = pl.BlockSpec(memory_space=pltpu.VMEM)
    in_smem = pl.BlockSpec(memory_space=pltpu.SMEM)
    in_place = pl.BlockSpec(memory_space=pl.ANY)

    packed, own_rope = pl.pallas_call(
        functools.partial(first_kernel, groups),
        out_shape=(
            jax.ShapeDtypeStruct((seq_count * rows, lanes), bf16),
            jax.ShapeDtypeStruct((block, 2 * rope_width), bf16),
        ),
        in_specs=[in_place] * 4,
        out_specs=(in_vmem, in_vmem),
        scratch_shapes=[
            pltpu.VMEM((2, local_blocks, rows, latent_width), bf16),
            pltpu.VMEM((2, local_blocks, rows, index_width), bf16),
            pltpu.VMEM((rope_width, local_blocks * block), bf16),
            pltpu.VMEM((local_blocks * block, 2 * rope_width), bf16),
            pltpu.VMEM((slot_count, seq_count), jnp.int32),
            pltpu.SemaphoreType.DMA((2 + 4 * local_blocks,)),
        ],
        compiler_params=pltpu.CompilerParams(vmem_limit_bytes=60 * 1024 * 1024),
    )(sel_blocks.T, latent_cache, rope_keys.T, index_keys)
    fetched = exchange(packed.reshape(seq_count, rows, lanes), "seq")

    share_rows = remote_slots * rows
    query_rows = tokens * heads
    index_rows = tokens * index_heads
    latent_parts = q_latent.reshape(block * heads, latent_width)
    rope_parts = q_rope.reshape(head_count, 2, query_rows // 2, rope_width)
    rope_parts = jnp.concatenate([rope_parts[:, 0], rope_parts[:, 1]], axis=-1)
    rope_parts = rope_parts.reshape(head_count * query_rows // 2, 2 * rope_width)
    index_parts = index_queries.reshape(head_count * index_rows, index_width)
    weight_parts = index_weights.reshape(head_count, 2, index_rows // 2, 1)
    high = lax.reduce_precision(weight_parts, 8, 7)
    middle = lax.reduce_precision(weight_parts - high, 8, 7)
    low = weight_parts - high - middle
    pieces = jnp.concatenate([high, middle, low], axis=-1).astype(bf16)
    pieces = pad_lanes(jnp.concatenate([pieces[:, 0], pieces[:, 1]], axis=-1), 128)
    pieces = pieces.reshape(head_count * index_rows // 2, 128)
    height = query_rows + index_rows + index_rows // 2
    total = slot_count * block
    axes = ("head", "seq")
    *parts, bias, key_bias = pl.pallas_call(
        functools.partial(query_kernel, side, groups),
        out_shape=tuple([jax.ShapeDtypeStruct((side, height, lanes), bf16)] * side)
        + (
            jax.ShapeDtypeStruct((tokens, total), f32),
            jax.ShapeDtypeStruct((total, 128), bf16),
        ),
        in_specs=[in_vmem] * 5,
        out_specs=tuple([in_vmem] * (side + 2)),
        compiler_params=pltpu.CompilerParams(vmem_limit_bytes=24 * 1024 * 1024),
    )(sel_blocks.T, latent_parts, rope_parts, index_parts, pieces)
    for k in range(1, side):
        parts[k] = lax.ppermute(parts[k], axes, shift_along_u(side, seq_count, k))
    outgoing = pl.pallas_call(
        functools.partial(stage_kernel, local_blocks),
        out_shape=jax.ShapeDtypeStruct((side, share_rows + side * height, lanes), bf16),
        in_specs=[in_smem] + [in_vmem] * (side + 1),
        out_specs=in_vmem,
        compiler_params=pltpu.CompilerParams(vmem_limit_bytes=24 * 1024 * 1024),
    )(sel_blocks.T, fetched, *parts)
    found = (source[1:][None, :] == jnp.arange(seq_count)[:, None]) & slot_valid[1:][None, :]
    slot_of = jnp.sum(jnp.where(found, jnp.arange(1, slot_count)[None, :], 0), axis=1)
    owner = wanted[:, None] & (which[:, None] == jnp.arange(local_blocks)[None, :])
    owner = owner.astype(f32)
    later = (bias, key_bias, own_rope, slot_of, owner)
    staged, later = exchange_alone(outgoing, axes, later, lines(side, seq_count, False))
    spread = pl.pallas_call(
        functools.partial(spread_kernel, share_rows),
        out_shape=jax.ShapeDtypeStruct((side, share_rows * 11 // 3, lanes), bf16),
        in_specs=[in_vmem],
        out_specs=in_vmem,
        compiler_params=pltpu.CompilerParams(vmem_limit_bytes=16 * 1024 * 1024),
    )(staged)
    spread, (staged, bias, key_bias, own_rope, slot_of, owner) = exchange_alone(
        spread, axes, (staged, *later), lines(side, seq_count, True)
    )

    all_rows = head_count * index_rows
    grad_queries, grad_weights, shares = pl.pallas_call(
        functools.partial(compute_kernel, loss_weight, index_scale, index_heads),
        out_shape=(
            jax.ShapeDtypeStruct((head_count, index_rows, index_width), bf16),
            jax.ShapeDtypeStruct((head_count, 16, 128), bf16),
            jax.ShapeDtypeStruct((head_count, slot_count * small, index_width), bf16),
        ),
        in_specs=[in_vmem] * 5 + [in_place] * 2,
        out_specs=(in_vmem, in_vmem, in_vmem),
        scratch_shapes=[
            pltpu.VMEM((total, latent_width + 256), bf16),
            pltpu.VMEM((total, index_width), bf16),
            pltpu.VMEM((head_count * query_rows, total), f32),
            pltpu.VMEM((head_count * query_rows, 128), f32),
            pltpu.VMEM((all_rows, total), f32),
            pltpu.VMEM((all_rows, total), f32),
            pltpu.VMEM((all_rows, total), bf16),
            pltpu.VMEM((index_rows, total), f32),
            pltpu.VMEM((query_rows, total), f32),
            pltpu.VMEM((total, index_width), f32),
            pltpu.SemaphoreType.DMA((2,)),
        ],
        compiler_params=pltpu.CompilerParams(vmem_limit_bytes=36 * 1024 * 1024),
    )(
        staged,
        spread,
        bias,
        key_bias,
        own_rope,
        latent_cache,
        index_keys,
    )

    collected, (grad_queries, grad_weights, slot_of, owner) = exchange_alone(
        shares, "head", (grad_queries, grad_weights, slot_of, owner)
    )
    summed = jnp.sum(collected.astype(f32), axis=0).reshape(slot_count, small, index_width)
    own_sum = summed[0]
    returned, (own_sum, grad_queries, grad_weights, owner) = exchange_alone(
        jnp.take(summed, slot_of, axis=0).astype(bf16),
        "seq",
        (own_sum, grad_queries, grad_weights, owner),
    )
    owned = jnp.sum(owner[:, :, None, None] * returned.astype(f32)[:, None], axis=0)
    owned = owned.at[local_blocks - 1].add(own_sum)

    own_rows = local_blocks * small
    last = jnp.concatenate(
        [
            jnp.broadcast_to(
                owned.reshape(own_rows, index_width).astype(bf16), (head_count, own_rows, index_width)
            ),
            grad_queries,
            grad_weights,
        ],
        axis=1,
    )
    final, _ = exchange_alone(last, "head", ())
    out_queries, out_weights, grad_keys = pl.pallas_call(
        functools.partial(last_kernel, groups, index_heads),
        out_shape=(
            jax.ShapeDtypeStruct((block * index_heads, index_width), f32),
            jax.ShapeDtypeStruct((index_heads, block), f32),
            jax.ShapeDtypeStruct((local_blocks * block, index_width), f32),
        ),
        in_specs=[in_vmem],
        out_specs=(in_vmem, in_vmem, in_vmem),
        compiler_params=pltpu.CompilerParams(vmem_limit_bytes=16 * 1024 * 1024),
    )(final)
    return (out_queries.reshape(block, index_heads, index_width), out_weights.T, grad_keys)


def solution(mesh):
    placed = (
        P("seq", "head", None),
        P("seq", "head", None),
        P("seq", None),
        P("seq", None),
        P("seq", "head", None),
        P("seq", "head"),
        P("seq", None),
        P(),
    )
    return jax.shard_map(
        body,
        mesh=mesh,
        in_specs=placed,
        out_specs=(P("seq", "head", None), P("seq", "head"), P("seq", None)),
        check_vma=False,
    )
```

```python
import functools
import math

import jax
import jax.numpy as jnp
from jax import lax
from jax.experimental import pallas as pl
from jax.experimental.pallas import tpu as pltpu
from jax.sharding import PartitionSpec as P

score_scale = 192.0 ** (-0.5)
gelu_coef = math.sqrt(2.0 / math.pi)
cubic_coef = 0.044715
bf16 = jnp.bfloat16
f32 = jnp.float32


def dot_last(a, b):
    return lax.dot_general(a, b, (((1,), (1,)), ((), ())), preferred_element_type=f32)


def dot(a, b, precision=None):
    return jnp.dot(a, b, preferred_element_type=f32, precision=precision)


def gelu_pair(values):
    square = values * values
    tangent = jnp.tanh(values * (gelu_coef + (gelu_coef * cubic_coef) * square))
    upper = 0.5 + 0.5 * tangent
    active = values * upper
    slope = upper + active * (1.0 - upper) * (
        2.0 * gelu_coef + (6.0 * gelu_coef * cubic_coef) * square
    )
    return (active, slope)


def first_kernel(
    groups,
    sel_turned,
    latent,
    rope_turned,
    index,
    packed,
    own_rope,
    wide,
    narrow,
    turned,
    rope,
    table,
    sems,
):
    slots, destinations = sel_turned.shape
    variants, local_blocks, rows, latent_width = wide.shape
    block = latent.shape[1]
    half_width = latent_width // 2
    side = groups // 2
    head = lax.axis_index("head")
    x, y = lax.div(head, side), lax.rem(head, side)
    firsts = []
    lows = []
    copies = [pltpu.make_async_copy(rope_turned, turned, sems.at[0])]
    table_copy = pltpu.make_async_copy(sel_turned, table, sems.at[1])
    table_copy.start()
    for i, (u, v) in enumerate(((y, x), (x, y))):
        first = pl.multiple_of((lax.rem(v, 2) * side + u) * rows, rows)
        at = pl.ds(first, rows)
        firsts.append(first)
        lows.append(v < side // 2)
        copies.append(pltpu.make_async_copy(latent.at[:, at], wide.at[i], sems.at[2 + i]))
        copies.append(
            pltpu.make_async_copy(index.at[:, at], narrow.at[i], sems.at[2 + variants + i])
        )
    for copy in copies:
        copy.start()

    total = packed.shape[0]
    repeat = lax.broadcasted_iota(jnp.int32, (total, destinations), 0) // rows
    repeat = (repeat == lax.broadcasted_iota(jnp.int32, (total, destinations), 1)).astype(f32)
    table_copy.wait()
    chosen = dot_last(repeat, table[...].astype(f32))
    offset = chosen - (lax.axis_index("seq") * local_blocks).astype(f32)
    slot = lax.broadcasted_iota(jnp.int32, (total, slots), 1)
    inside = (chosen >= 0) & (offset >= 0) & (offset < local_blocks) & (slot > 0)
    which = jnp.sum(jnp.where(inside, offset, 0.0), axis=1, keepdims=True)
    width = variants * local_blocks * rows
    row = lax.broadcasted_iota(jnp.int32, (total, width), 0)
    start = (row // rows) % variants * (local_blocks * rows) + row % rows
    column = lax.broadcasted_iota(jnp.int32, (total, width), 1)
    pick = (column.astype(f32) == which * rows + start.astype(f32)).astype(bf16)

    for copy in copies:
        copy.wait()
    rope_rows = turned[...].astype(f32)
    rope[...] = jnp.concatenate([rope_rows, rope_rows], axis=0).T.astype(bf16)
    parts = []
    for i in range(variants):
        for k in range(local_blocks):
            parts.append(
                jnp.concatenate(
                    [
                        jnp.where(lows[i], wide[i, k, :, 0:half_width], wide[i, k, :, half_width:]),
                        jnp.where(
                            lows[i],
                            narrow[i, k],
                            rope[pl.ds(pl.multiple_of(k * block + firsts[i], rows), rows), :],
                        ),
                    ],
                    axis=1,
                )
            )
    own_rope[...] = rope[(local_blocks - 1) * block :, :]
    share = jnp.concatenate(parts, axis=0)
    packed[...] = dot(pick, share).astype(bf16)


def place(side):
    head = lax.axis_index("head")
    core = lax.rem(lax.axis_index("seq"), 2)
    x, y = lax.div(head, side), lax.rem(head, side)
    return core, jnp.where(core == 0, y, x), jnp.where(core == 0, x, y)


def head_at(side, core, u, v):
    return jnp.where(core == 0, v * side + u, u * side + v)


def query_kernel(
    side, groups, sel_turned, latent, rope, index, weight, out0, out1, out2, out3, bias, key_bias
):
    outs = (out0, out1, out2, out3)
    chunks = side * side
    slots, destinations = sel_turned.shape
    query_rows = latent.shape[0] // chunks
    lanes = out0.shape[2]
    index_rows = index.shape[0] // chunks
    rope_rows = rope.shape[0] // chunks
    weight_rows = weight.shape[0] // chunks
    tall = index_rows + weight_rows
    rest = query_rows - tall
    core, u, _ = place(side)
    for k in range(side):
        out = outs[k]
        for v in range(side):
            chunk = head_at(side, core, lax.rem(u + k, side), v)

            def at(count, size, begin=0):
                return pl.ds(pl.multiple_of(chunk * count + begin, 16), size)

            out[v, 0:query_rows, :] = latent[at(query_rows, query_rows), 0:lanes]
            out[v, query_rows : query_rows + tall, 0:128] = latent[at(query_rows, tall), lanes:]
            out[v, query_rows : query_rows + rest, 128:256] = latent[
                at(query_rows, rest, tall), lanes:
            ]
            out[v, query_rows + rest : query_rows + tall, 128:256] = rope[
                at(rope_rows, rope_rows), :
            ]
            out[v, query_rows : query_rows + index_rows, 256:384] = index[
                at(index_rows, index_rows), :
            ]
            out[v, query_rows + index_rows : query_rows + tall, 256:384] = weight[
                at(weight_rows, weight_rows), :
            ]
    tokens, total = bias.shape
    rows = total // slots // groups
    share_rows = (slots - 1) * rows
    remote = groups * share_rows
    here = lax.axis_index("seq")
    head = lax.axis_index("head")
    table = sel_turned[...].astype(f32)
    pick = lax.broadcasted_iota(jnp.int32, (tokens, destinations), 1) == here
    valid = (dot_last(pick.astype(f32), table) >= 0).astype(f32)
    key = lax.broadcasted_iota(jnp.int32, (slots, total), 1)
    slot = lax.div(lax.rem(key, share_rows), rows) + 1
    mark = (slot == lax.broadcasted_iota(jnp.int32, (slots, total), 0)).astype(f32)
    key = lax.broadcasted_iota(jnp.int32, (tokens, total), 1)
    token = lax.broadcasted_iota(jnp.int32, (tokens, total), 0) + head * tokens
    good = ((key < remote) & (dot(valid, mark) > 0)) | ((key >= remote) & (key - remote <= token))
    masks = jnp.where(good, 0.0, -1e30)
    bias[...] = masks
    tall_masks = jnp.concatenate([masks, jnp.zeros((128 - tokens, total), f32)], axis=0)
    key_bias[...] = tall_masks.T.astype(bf16)


def stage_kernel(local_blocks, sel, fetched, in0, in1, in2, in3, outgoing):
    parts = (in0, in1, in2, in3)
    slots = sel.shape[0]
    rows = fetched.shape[1]
    height = in0.shape[1]
    here = lax.axis_index("seq")
    first = (slots - 1) * rows
    for j in range(1, slots):
        piece = fetched[lax.div(jnp.maximum(sel[j, here], 0), local_blocks)]
        for v in range(len(parts)):
            outgoing[v, (j - 1) * rows : j * rows, :] = piece
    for k in range(len(parts)):
        for v in range(len(parts)):
            at = first + k * height
            outgoing[v, at : at + height, :] = parts[k][v]


def spread_kernel(share, staged, outgoing):
    side = outgoing.shape[0]
    lane_low = (lax.broadcasted_iota(jnp.int32, (share, 128), 1) < 64).astype(f32)
    third, fourth = staged[2, 0:share, :], staged[3, 0:share, :]
    rope = third[:, 256:384] * lane_low.astype(bf16) + fourth[:, 256:384] * (
        1.0 - lane_low
    ).astype(bf16)
    long = share * 2 // 3
    rest = share - long
    for u in range(side):
        outgoing[u, 0:share, :] = staged[0, 0:share, :]
        outgoing[u, share : 2 * share, :] = staged[1, 0:share, :]
        outgoing[u, 2 * share : 3 * share, 0:256] = third[:, 0:256]
        outgoing[u, 2 * share : 3 * share, 256:384] = rope
        at = 3 * share
        outgoing[u, at : at + long, 0:256] = fourth[0:long, 0:256]
        outgoing[u, at : at + rest, 256:384] = fourth[long:, 0:128]
        outgoing[u, at + rest : at + long, 256:384] = fourth[long:, 128:256]


def compute_kernel(
    loss_weight,
    index_scale,
    index_heads,
    staged,
    spread_shares,
    bias,
    key_bias,
    own_rope,
    latent,
    index,
    grad_queries,
    grad_weights,
    shares,
    keys,
    index_k,
    scores,
    highest,
    active,
    slope,
    grad_pre,
    logit_rows,
    target_rows,
    grad_keys,
    sems,
):
    step = staged.shape[0]
    sources = step * step
    groups = sources // 2
    tokens, total = bias.shape
    block = own_rope.shape[0]
    latent_width = latent.shape[1]
    half_width = latent_width // 2
    index_width = index.shape[1]
    query_rows = target_rows.shape[0]
    heads = query_rows // tokens
    index_rows = logit_rows.shape[0]
    remote = total - block
    share_rows = remote // groups
    tile = 2 * 128
    tiles = total // tile
    score_rows = step * query_rows
    chunk = step * index_rows
    height = (staged.shape[1] - share_rows) // step
    tall = height - query_rows
    rest = query_rows - tall
    core, own_u, _ = place(step)
    own_rows = pl.ds(latent.shape[0] - block, block)
    copies = (
        pltpu.make_async_copy(
            latent.at[own_rows], keys.at[pl.ds(remote, block), pl.ds(0, latent_width)], sems.at[0]
        ),
        pltpu.make_async_copy(index.at[own_rows], index_k.at[pl.ds(remote, block)], sems.at[1]),
    )
    for copy in copies:
        copy.start()

    long = share_rows * 2 // 3
    short = share_rows - long
    last = 3 * share_rows
    under = lax.broadcasted_iota(jnp.int32, (share_rows, 128), 1) < 64
    middle_lanes = slice(half_width, latent_width)
    rope_lanes = slice(latent_width, latent_width + 128)

    def gather_keys(g):
        i, u = g // step, g % step
        at = slice(g * share_rows, (g + 1) * share_rows)
        low = slice(i * share_rows, (i + 1) * share_rows)
        keys[at, 0:half_width] = spread_shares[u, low, 0:half_width]
        index_k[at, :] = spread_shares[u, low, half_width:]
        rope = spread_shares[u, 2 * share_rows : last, half_width:].astype(f32)
        swapped = pltpu.roll(rope, 64, 1)
        if i == 0:
            keys[at, middle_lanes] = spread_shares[u, 2 * share_rows : last, 0:half_width]
            keys[at, rope_lanes] = jnp.where(under, rope, swapped).astype(bf16)
        else:
            top = slice(g * share_rows, g * share_rows + long)
            end = slice(g * share_rows + long, (g + 1) * share_rows)
            keys[top, middle_lanes] = spread_shares[u, last : last + long, 0:half_width]
            keys[end, middle_lanes] = jnp.concatenate(
                [
                    spread_shares[u, last : last + short, half_width:],
                    spread_shares[u, last + short : last + long, half_width:],
                ],
                axis=1,
            )
            keys[at, rope_lanes] = jnp.where(under, swapped, rope).astype(bf16)

    keys[remote:total, latent_width : latent_width + 128] = own_rope[...]
    keys[:, latent_width + 128 :] = key_bias[...]
    target_rows[...] = jnp.zeros_like(target_rows)
    logit_rows[...] = jnp.zeros_like(logit_rows)
    for copy in copies:
        copy.wait()

    lane_low = lax.broadcasted_iota(jnp.int32, (query_rows // 2, 128), 1) < 64
    lane_low = lane_low.astype(f32)
    keep_low = lane_low.astype(bf16)
    keep_high = (1.0 - lane_low).astype(bf16)

    on_token = (
        lax.broadcasted_iota(jnp.int32, (query_rows, 128), 0) // heads
        == lax.broadcasted_iota(jnp.int32, (query_rows, 128), 1)
    ).astype(bf16)

    def queries_of(v):
        pieces = []
        for k in range(step):
            at = share_rows + k * height
            below = at + query_rows
            rope = staged[v, below + rest : below + tall, 128:256]
            pieces.append(
                jnp.concatenate(
                    [
                        staged[v, at:below, :],
                        jnp.concatenate(
                            [
                                staged[v, below : below + tall, 0:128],
                                staged[v, below : below + rest, 128:256],
                            ],
                            axis=0,
                        ),
                        jnp.concatenate([rope * keep_low, rope * keep_high], axis=0),
                        on_token,
                    ],
                    axis=1,
                )
            )
        return jnp.concatenate(pieces, axis=0)

    def index_queries_of(v):
        pieces = []
        for k in range(step):
            below = share_rows + k * height + query_rows
            pieces.append(staged[v, below : below + index_rows, 256:384])
        return jnp.concatenate(pieces, axis=0)

    def weights_of(v):
        columns = []
        for k in range(step):
            below = share_rows + k * height + query_rows
            pieces = staged[v, below + index_rows : below + tall, 256:384].astype(f32)
            early = lax.broadcasted_iota(jnp.int32, pieces.shape, 1) < 3
            columns.append(jnp.sum(jnp.where(early, pieces, 0.0), axis=1, keepdims=True))
            columns.append(jnp.sum(jnp.where(early, 0.0, pieces), axis=1, keepdims=True))
        return jnp.concatenate(columns, axis=0).reshape(step, index_rows, 1)

    def source_of(v, k):
        return head_at(step, core, lax.rem(own_u + step - k, step), v)

    tile_at = [slice(k * tile, (k + 1) * tile) for k in range(tiles)]

    def soften(c, state, k):
        score_at = slice(c * score_rows, (c + 1) * score_rows)
        if k == 0:
            state["top"] = jnp.max(state["best"], axis=1, keepdims=True)
            state["sums"] = jnp.zeros((score_rows, 128), f32)
        if k == tiles // 2:
            weight = 1.0 / ((heads * sources) * jnp.sum(state["sums"], axis=1, keepdims=True))
            state["weight"] = weight.reshape(step, query_rows, 1)
        for i in range(2):
            if k < tiles // 2:
                at = tile_at[2 * k + i]
                power = jnp.exp((scores[score_at, at] - state["top"]) * score_scale)
                scores[score_at, at] = power
                state["sums"] = state["sums"] + (power[:, 0:128] + power[:, 128:256])
            else:
                at = tile_at[2 * k - tiles + i]
                power = scores[score_at, at].reshape(step, query_rows, tile)
                target_rows[:, at] += jnp.sum(power * state["weight"], axis=0)

    state = None
    ready = 0
    for c in range(sources // step):
        score_at = slice(c * score_rows, (c + 1) * score_rows)
        rows = slice(c * chunk, (c + 1) * chunk)
        queries = queries_of(c)
        index_q = index_queries_of(c)
        weights = weights_of(c)
        best = jnp.full((score_rows, 128), -3e38, f32)
        for k in range(tiles):
            at = tile_at[k]
            while c == 0 and ready < min((k + 1) * tile, remote):
                gather_keys(ready // share_rows)
                ready += share_rows
            part = dot_last(queries, keys[at, :])
            scores[score_at, at] = part
            best = jnp.maximum(best, jnp.maximum(part[:, 0:128], part[:, 128:256]))
            act, rate = gelu_pair(dot_last(index_q, index_k[at, :]) * index_scale)
            active[rows, at] = act
            slope[rows, at] = rate
            logit_rows[:, at] += jnp.sum(
                act.reshape(step, index_rows, tile) * weights, axis=0
            )
            if state is not None:
                soften(c - 1, state, k)
        state = {"best": best}
    for k in range(tiles):
        soften(sources // step - 1, state, k)

    def gather(count):
        return (
            lax.broadcasted_iota(jnp.int32, (tokens, tokens * count), 1) // count
            == lax.broadcasted_iota(jnp.int32, (tokens, tokens * count), 0)
        ).astype(f32)

    spread = (
        lax.broadcasted_iota(jnp.int32, (index_rows, tokens), 0) // index_heads
        == lax.broadcasted_iota(jnp.int32, (index_rows, tokens), 1)
    ).astype(bf16)
    logits = dot(gather(index_heads), logit_rows[...], lax.Precision.HIGHEST) + bias[...]
    target = dot(gather(heads), target_rows[...], lax.Precision.HIGHEST)
    likely = jnp.exp(logits - jnp.max(logits, axis=1, keepdims=True))
    predicted = likely / jnp.sum(likely, axis=1, keepdims=True)
    grad_logits = jnp.where(
        bias[...] == 0.0, loss_weight * (predicted - target), 0.0
    ).astype(bf16)
    logit_rows[...] = dot(spread, grad_logits)

    for c in range(sources // step):
        rows = slice(c * chunk, (c + 1) * chunk)
        weights = weights_of(c) * index_scale
        sums = jnp.zeros((chunk, 128), f32)
        for k in range(tiles):
            at = slice(k * tile, (k + 1) * tile)
            grad = logit_rows[:, at][None]
            product = (
                active[rows, at].reshape(step, index_rows, tile) * grad
            ).reshape(chunk, tile)
            sums = sums + (product[:, 0:128] + product[:, 128:256])
            grad_pre[rows, at] = (
                (slope[rows, at].reshape(step, index_rows, tile) * (grad * weights))
                .reshape(chunk, tile)
                .astype(bf16)
            )
        turned = jnp.broadcast_to(jnp.sum(sums, axis=1, keepdims=True), (chunk, 128)).T
        for k in range(step):
            own = turned[0:8] if k == 0 else pltpu.roll(turned[0:8], 128 - k * index_rows, 1)
            own_high = own.astype(bf16)
            own_low = (own - own_high.astype(f32)).astype(bf16)
            grad_weights[source_of(c, k)] = jnp.concatenate([own_high, own_low], axis=0)

    result = dot(grad_pre[...], index_k[...]).astype(bf16)
    for v in range(step):
        for k in range(step):
            at = (v * step + k) * index_rows
            grad_queries[source_of(v, k)] = result[at : at + index_rows]
    turned = jnp.concatenate([index_queries_of(v) for v in range(step)], axis=0)
    turned = turned.astype(f32).T.astype(bf16)
    for k in range(tiles):
        at = slice(k * tile, (k + 1) * tile)
        grad_keys[at, :] = dot(turned, grad_pre[:, at]).T
    small = block // sources
    slots = total // block
    for g in range(groups):
        own = grad_keys[remote + g * 2 * small : remote + (g + 1) * 2 * small, :]
        own = own.reshape(1, 2, small, index_width)
        rest_keys = grad_keys[g * share_rows : (g + 1) * share_rows, :]
        rest_keys = rest_keys.reshape(slots - 1, 2, small, index_width)
        both_keys = jnp.concatenate([own, rest_keys], axis=0)
        for i in range(2):
            shares[i * groups + g] = both_keys[:, i].reshape(block, index_width).astype(bf16)


def route_kernel(local_blocks, sel_turned, collected, outgoing, own_sum):
    slots, owners = sel_turned.shape
    total, width = outgoing.shape[0], collected.shape[1]
    small = total // owners
    summed = collected[0].astype(f32)
    for k in range(1, collected.shape[0]):
        summed = summed + collected[k].astype(f32)
    own_sum[...] = summed[0:small]
    here = lax.axis_index("seq")
    pick = (lax.broadcasted_iota(jnp.int32, (total, owners), 1) == here).astype(f32)
    blocks = dot_last(pick, sel_turned[...].astype(f32))
    slot = lax.broadcasted_iota(jnp.int32, (slots, width), 1) // small
    mark = (slot == lax.broadcasted_iota(jnp.int32, (slots, width), 0)).astype(f32)
    block = dot(blocks, mark)
    row = lax.broadcasted_iota(jnp.int32, (total, width), 0)
    column = lax.broadcasted_iota(jnp.int32, (total, width), 1)
    first = (row // small * local_blocks).astype(f32)
    chosen = (block >= first) & (block < first + local_blocks)
    chosen = chosen & (column >= small) & (column % small == row % small)
    outgoing[...] = dot(chosen.astype(bf16), summed.astype(bf16)).astype(bf16)


def last_kernel(groups, index_heads, final, grad_queries, grad_weights, grad_keys):
    sources, _, width = final.shape
    block = grad_weights.shape[1]
    tokens = block // sources
    index_rows = tokens * index_heads
    local_blocks = grad_keys.shape[0] // block
    small = block // sources
    own_rows = local_blocks * small
    second = own_rows + index_rows
    for k in range(sources):
        part = final[k, 0:own_rows, :].astype(f32)
        half, group = k // groups, k % groups
        for j in range(local_blocks):
            at = j * block + group * 2 * small + half * small
            grad_keys[at : at + small, :] = part[j * small : (j + 1) * small]
        grad_queries[k * index_rows : (k + 1) * index_rows, :] = final[
            k, own_rows:second, :
        ].astype(f32)
    row = lax.broadcasted_iota(jnp.int32, (block, width), 0)
    lane = lax.broadcasted_iota(jnp.int32, (block, width), 1)
    keep = (lane < index_rows) & (lax.div(lane, index_heads) == row % tokens)
    which = lax.broadcasted_iota(jnp.int32, (8, width), 0)
    head = lax.rem(lax.broadcasted_iota(jnp.int32, (8, width), 1), index_heads)
    fold = (which == head).astype(bf16)
    result = jnp.zeros((8, block), f32)
    for i in range(2):
        lines = []
        for k in range(sources):
            whole = final[k, second : second + 16, :].astype(f32)
            lines.append(jnp.broadcast_to(whole[8 * i : 8 * i + 1], (tokens, width)))
        lines = jnp.concatenate(lines, axis=0)
        result = result + dot_last(fold, jnp.where(keep, lines, 0.0).astype(bf16))
    grad_weights[...] = result[0:index_heads]


def exchange(array, axis, groups=None):
    return lax.all_to_all(
        array, axis, split_axis=0, concat_axis=0, tiled=True, axis_index_groups=groups
    )


def exchange_alone(array, axis, others, groups=None):
    array, others = lax.optimization_barrier((array, others))
    return lax.optimization_barrier((exchange(array, axis, groups), others))


def flat_index(side, seq_count, u, v, seq):
    x, y = (v, u) if seq % 2 == 0 else (u, v)
    return (x * side + y) * seq_count + seq


def lines(side, seq_count, along_u):
    return [
        [
            flat_index(side, seq_count, *((i, j) if along_u else (j, i)), seq)
            for i in range(side)
        ]
        for seq in range(seq_count)
        for j in range(side)
    ]


def shift_along_u(side, seq_count, k):
    return [
        (
            flat_index(side, seq_count, u, v, seq),
            flat_index(side, seq_count, (u + k) % side, v, seq),
        )
        for seq in range(seq_count)
        for u in range(side)
        for v in range(side)
    ]


def pad_lanes(array, width):
    return jnp.pad(array, [(0, 0)] * (array.ndim - 1) + [(0, width - array.shape[-1])])


def body(
    q_latent, q_rope, latent_cache, rope_keys, index_queries, index_weights, index_keys, sel_blocks
):
    head_count = lax.axis_size("head")
    seq_count = lax.axis_size("seq")
    head_index = lax.axis_index("head")
    seq_index = lax.axis_index("seq")
    block, heads, latent_width = q_latent.shape
    rope_width = q_rope.shape[2]
    index_heads, index_width = index_queries.shape[1:]
    slot_count = sel_blocks.shape[1]
    local_blocks = latent_cache.shape[0] // block
    index_scale = index_width ** (-0.5)
    loss_weight = float(slot_count * block)
    groups = head_count // 2
    side = math.isqrt(head_count)
    rows = block // groups
    small = rows // 2
    tokens = block // head_count
    half_width = latent_width // 2
    lanes = half_width + index_width
    remote_slots = slot_count - 1

    later = sel_blocks[:, 1:]
    offsets = later - seq_index * local_blocks
    inside = (later >= 0) & (offsets >= 0) & (offsets < local_blocks)
    wanted = jnp.any(inside, axis=1)
    which = jnp.sum(jnp.where(inside, offsets, 0), axis=1)
    in_vmem = pl.BlockSpec(memory_space=pltpu.VMEM)
    in_smem = pl.BlockSpec(memory_space=pltpu.SMEM)
    in_place = pl.BlockSpec(memory_space=pl.ANY)

    packed, own_rope = pl.pallas_call(
        functools.partial(first_kernel, groups),
        out_shape=(
            jax.ShapeDtypeStruct((seq_count * rows, lanes), bf16),
            jax.ShapeDtypeStruct((block, 2 * rope_width), bf16),
        ),
        in_specs=[in_place] * 4,
        out_specs=(in_vmem, in_vmem),
        scratch_shapes=[
            pltpu.VMEM((2, local_blocks, rows, latent_width), bf16),
            pltpu.VMEM((2, local_blocks, rows, index_width), bf16),
            pltpu.VMEM((rope_width, local_blocks * block), bf16),
            pltpu.VMEM((local_blocks * block, 2 * rope_width), bf16),
            pltpu.VMEM((slot_count, seq_count), jnp.int32),
            pltpu.SemaphoreType.DMA((6,)),
        ],
        compiler_params=pltpu.CompilerParams(vmem_limit_bytes=60 * 1024 * 1024),
    )(
        sel_blocks.T,
        latent_cache.reshape(local_blocks, block, latent_width),
        rope_keys.T,
        index_keys.reshape(local_blocks, block, index_width),
    )
    fetched = exchange(packed.reshape(seq_count, rows, lanes), "seq")

    share_rows = remote_slots * rows
    query_rows = tokens * heads
    index_rows = tokens * index_heads
    latent_parts = q_latent.reshape(block * heads, latent_width)
    rope_parts = q_rope.reshape(head_count, 2, query_rows // 2, rope_width)
    rope_parts = jnp.concatenate([rope_parts[:, 0], rope_parts[:, 1]], axis=-1)
    rope_parts = rope_parts.reshape(head_count * query_rows // 2, 2 * rope_width)
    index_parts = index_queries.reshape(head_count * index_rows, index_width)
    weight_parts = index_weights.reshape(head_count, 2, index_rows // 2, 1)
    high = lax.reduce_precision(weight_parts, 8, 7)
    middle = lax.reduce_precision(weight_parts - high, 8, 7)
    low = weight_parts - high - middle
    pieces = jnp.concatenate([high, middle, low], axis=-1).astype(bf16)
    pieces = pad_lanes(jnp.concatenate([pieces[:, 0], pieces[:, 1]], axis=-1), 128)
    pieces = pieces.reshape(head_count * index_rows // 2, 128)
    height = query_rows + index_rows + index_rows // 2
    total = slot_count * block
    axes = ("head", "seq")
    *parts, bias, key_bias = pl.pallas_call(
        functools.partial(query_kernel, side, groups),
        out_shape=tuple([jax.ShapeDtypeStruct((side, height, lanes), bf16)] * side)
        + (
            jax.ShapeDtypeStruct((tokens, total), f32),
            jax.ShapeDtypeStruct((total, 128), bf16),
        ),
        in_specs=[in_vmem] * 5,
        out_specs=tuple([in_vmem] * (side + 2)),
        compiler_params=pltpu.CompilerParams(vmem_limit_bytes=24 * 1024 * 1024),
    )(sel_blocks.T, latent_parts, rope_parts, index_parts, pieces)
    for k in range(1, side):
        parts[k] = lax.ppermute(parts[k], axes, shift_along_u(side, seq_count, k))
    outgoing = pl.pallas_call(
        functools.partial(stage_kernel, local_blocks),
        out_shape=jax.ShapeDtypeStruct((side, share_rows + side * height, lanes), bf16),
        in_specs=[in_smem] + [in_vmem] * (side + 1),
        out_specs=in_vmem,
        compiler_params=pltpu.CompilerParams(vmem_limit_bytes=24 * 1024 * 1024),
    )(sel_blocks.T, fetched, *parts)
    owner = wanted[:, None] & (which[:, None] == jnp.arange(local_blocks)[None, :])
    owner = owner.astype(f32)
    later = (bias, key_bias, own_rope, owner)
    staged, later = exchange_alone(outgoing, axes, later, lines(side, seq_count, False))
    spread = pl.pallas_call(
        functools.partial(spread_kernel, share_rows),
        out_shape=jax.ShapeDtypeStruct((side, share_rows * 11 // 3, lanes), bf16),
        in_specs=[in_vmem],
        out_specs=in_vmem,
        compiler_params=pltpu.CompilerParams(vmem_limit_bytes=16 * 1024 * 1024),
    )(staged)
    spread, (staged, bias, key_bias, own_rope, owner) = exchange_alone(
        spread, axes, (staged, *later), lines(side, seq_count, True)
    )

    all_rows = head_count * index_rows
    grad_queries, grad_weights, shares = pl.pallas_call(
        functools.partial(compute_kernel, loss_weight, index_scale, index_heads),
        out_shape=(
            jax.ShapeDtypeStruct((head_count, index_rows, index_width), bf16),
            jax.ShapeDtypeStruct((head_count, 16, 128), bf16),
            jax.ShapeDtypeStruct((head_count, slot_count * small, index_width), bf16),
        ),
        in_specs=[in_vmem] * 5 + [in_place] * 2,
        out_specs=(in_vmem, in_vmem, in_vmem),
        scratch_shapes=[
            pltpu.VMEM((total, latent_width + 256), bf16),
            pltpu.VMEM((total, index_width), bf16),
            pltpu.VMEM((head_count * query_rows, total), f32),
            pltpu.VMEM((head_count * query_rows, 128), f32),
            pltpu.VMEM((all_rows, total), f32),
            pltpu.VMEM((all_rows, total), f32),
            pltpu.VMEM((all_rows, total), bf16),
            pltpu.VMEM((index_rows, total), f32),
            pltpu.VMEM((query_rows, total), f32),
            pltpu.VMEM((total, index_width), f32),
            pltpu.SemaphoreType.DMA((2,)),
        ],
        compiler_params=pltpu.CompilerParams(vmem_limit_bytes=36 * 1024 * 1024),
    )(
        staged,
        spread,
        bias,
        key_bias,
        own_rope,
        latent_cache,
        index_keys,
    )

    collected, (grad_queries, grad_weights, owner) = exchange_alone(
        shares, "head", (grad_queries, grad_weights, owner)
    )
    routed, own_sum = pl.pallas_call(
        functools.partial(route_kernel, local_blocks),
        out_shape=(
            jax.ShapeDtypeStruct((seq_count * small, index_width), bf16),
            jax.ShapeDtypeStruct((small, index_width), f32),
        ),
        in_specs=[in_vmem, in_vmem],
        out_specs=(in_vmem, in_vmem),
        compiler_params=pltpu.CompilerParams(vmem_limit_bytes=16 * 1024 * 1024),
    )(sel_blocks.T, collected)
    returned, (own_sum, grad_queries, grad_weights, owner) = exchange_alone(
        routed.reshape(seq_count, small, index_width),
        "seq",
        (own_sum, grad_queries, grad_weights, owner),
    )
    owned = jnp.sum(owner[:, :, None, None] * returned.astype(f32)[:, None], axis=0)
    owned = owned.at[local_blocks - 1].add(own_sum)

    own_rows = local_blocks * small
    last = jnp.concatenate(
        [
            jnp.broadcast_to(
                owned.reshape(own_rows, index_width).astype(bf16), (head_count, own_rows, index_width)
            ),
            grad_queries,
            grad_weights,
        ],
        axis=1,
    )
    final, _ = exchange_alone(last, "head", ())
    out_queries, out_weights, grad_keys = pl.pallas_call(
        functools.partial(last_kernel, groups, index_heads),
        out_shape=(
            jax.ShapeDtypeStruct((block * index_heads, index_width), f32),
            jax.ShapeDtypeStruct((index_heads, block), f32),
            jax.ShapeDtypeStruct((local_blocks * block, index_width), f32),
        ),
        in_specs=[in_vmem],
        out_specs=(in_vmem, in_vmem, in_vmem),
        compiler_params=pltpu.CompilerParams(vmem_limit_bytes=16 * 1024 * 1024),
    )(final)
    return (out_queries.reshape(block, index_heads, index_width), out_weights.T, grad_keys)


def solution(mesh):
    placed = (
        P("seq", "head", None),
        P("seq", "head", None),
        P("seq", None),
        P("seq", None),
        P("seq", "head", None),
        P("seq", "head"),
        P("seq", None),
        P(),
    )
    return jax.shard_map(
        body,
        mesh=mesh,
        in_specs=placed,
        out_specs=(P("seq", "head", None), P("seq", "head"), P("seq", None)),
        check_vma=False,
    )
```

```python
import functools
import math

import jax
import jax.numpy as jnp
from jax import lax
from jax.experimental import pallas as pl
from jax.experimental.pallas import tpu as pltpu
from jax.sharding import PartitionSpec as P

score_scale = 192.0 ** (-0.5)
gelu_coef = math.sqrt(2.0 / math.pi)
cubic_coef = 0.044715
bf16 = jnp.bfloat16
f32 = jnp.float32


def dot_last(a, b):
    return lax.dot_general(a, b, (((1,), (1,)), ((), ())), preferred_element_type=f32)


def dot(a, b, precision=None):
    return jnp.dot(a, b, preferred_element_type=f32, precision=precision)


def gelu_pair(values):
    square = values * values
    tangent = jnp.tanh(values * (gelu_coef + (gelu_coef * cubic_coef) * square))
    upper = 0.5 + 0.5 * tangent
    active = values * upper
    slope = upper + active * (1.0 - upper) * (
        2.0 * gelu_coef + (6.0 * gelu_coef * cubic_coef) * square
    )
    return (active, slope)


def first_kernel(
    groups,
    sel_turned,
    latent,
    rope_turned,
    index,
    packed,
    wide,
    narrow,
    turned,
    table,
    sems,
):
    slots, destinations = sel_turned.shape
    variants, local_blocks, rows, latent_width = wide.shape
    block = latent.shape[1]
    half_width = latent_width // 2
    side = groups // 2
    head = lax.axis_index("head")
    x, y = lax.div(head, side), lax.rem(head, side)
    firsts = []
    lows = []
    copies = [pltpu.make_async_copy(rope_turned, turned, sems.at[0])]
    table_copy = pltpu.make_async_copy(sel_turned, table, sems.at[1])
    table_copy.start()
    for i, (u, v) in enumerate(((y, x), (x, y))):
        first = pl.multiple_of((lax.rem(v, 2) * side + u) * rows, rows)
        at = pl.ds(first, rows)
        firsts.append(first)
        lows.append(v < side // 2)
        copies.append(pltpu.make_async_copy(latent.at[:, at], wide.at[i], sems.at[2 + i]))
        copies.append(
            pltpu.make_async_copy(index.at[:, at], narrow.at[i], sems.at[2 + variants + i])
        )
    for copy in copies:
        copy.start()

    total = packed.shape[0]
    repeat = lax.broadcasted_iota(jnp.int32, (total, destinations), 0) // rows
    repeat = (repeat == lax.broadcasted_iota(jnp.int32, (total, destinations), 1)).astype(f32)
    table_copy.wait()
    chosen = dot_last(repeat, table[...].astype(f32))
    offset = chosen - (lax.axis_index("seq") * local_blocks).astype(f32)
    slot = lax.broadcasted_iota(jnp.int32, (total, slots), 1)
    inside = (chosen >= 0) & (offset >= 0) & (offset < local_blocks) & (slot > 0)
    which = jnp.sum(jnp.where(inside, offset, 0.0), axis=1, keepdims=True)
    width = variants * local_blocks * rows
    row = lax.broadcasted_iota(jnp.int32, (total, width), 0)
    start = (row // rows) % variants * (local_blocks * rows) + row % rows
    column = lax.broadcasted_iota(jnp.int32, (total, width), 1)
    pick = (column.astype(f32) == which * rows + start.astype(f32)).astype(bf16)

    tokens = rope_turned.shape[1]
    row = lax.broadcasted_iota(jnp.int32, (width, tokens), 0)
    spot = (row // rows) % local_blocks * block + row % rows
    spot = spot + jnp.where(row < local_blocks * rows, firsts[0], firsts[1])
    spot = (spot == lax.broadcasted_iota(jnp.int32, (width, tokens), 1)).astype(bf16)

    for copy in copies:
        copy.wait()
    rope = dot_last(spot, jnp.concatenate([turned[...], turned[...]], axis=0)).astype(bf16)
    parts = []
    for i in range(variants):
        for k in range(local_blocks):
            parts.append(
                jnp.concatenate(
                    [
                        jnp.where(lows[i], wide[i, k, :, 0:half_width], wide[i, k, :, half_width:]),
                        jnp.where(
                            lows[i],
                            narrow[i, k],
                            rope[(i * local_blocks + k) * rows : (i * local_blocks + k + 1) * rows],
                        ),
                    ],
                    axis=1,
                )
            )
    share = jnp.concatenate(parts, axis=0)
    packed[...] = dot(pick, share).astype(bf16)


def place(side):
    head = lax.axis_index("head")
    core = lax.rem(lax.axis_index("seq"), 2)
    x, y = lax.div(head, side), lax.rem(head, side)
    return core, jnp.where(core == 0, y, x), jnp.where(core == 0, x, y)


def head_at(side, core, u, v):
    return jnp.where(core == 0, v * side + u, u * side + v)


def query_kernel(
    side, groups, sel_turned, latent, rope, index, weight, out0, out1, out2, out3, bias, key_bias
):
    outs = (out0, out1, out2, out3)
    chunks = side * side
    slots, destinations = sel_turned.shape
    query_rows = latent.shape[0] // chunks
    lanes = out0.shape[2]
    index_rows = index.shape[0] // chunks
    rope_rows = rope.shape[0] // chunks
    weight_rows = weight.shape[0] // chunks
    tall = index_rows + weight_rows
    rest = query_rows - tall
    core, u, _ = place(side)
    for k in range(side):
        out = outs[k]
        for v in range(side):
            chunk = head_at(side, core, lax.rem(u + k, side), v)

            def at(count, size, begin=0):
                return pl.ds(pl.multiple_of(chunk * count + begin, 16), size)

            out[v, 0:query_rows, :] = latent[at(query_rows, query_rows), 0:lanes]
            out[v, query_rows : query_rows + tall, 0:128] = latent[at(query_rows, tall), lanes:]
            out[v, query_rows : query_rows + rest, 128:256] = latent[
                at(query_rows, rest, tall), lanes:
            ]
            out[v, query_rows + rest : query_rows + tall, 128:256] = rope[
                at(rope_rows, rope_rows), :
            ]
            out[v, query_rows : query_rows + index_rows, 256:384] = index[
                at(index_rows, index_rows), :
            ]
            out[v, query_rows + index_rows : query_rows + tall, 256:384] = weight[
                at(weight_rows, weight_rows), :
            ]
    tokens, total = bias.shape
    rows = total // slots // groups
    share_rows = (slots - 1) * rows
    remote = groups * share_rows
    here = lax.axis_index("seq")
    head = lax.axis_index("head")
    table = sel_turned[...].astype(f32)
    pick = lax.broadcasted_iota(jnp.int32, (tokens, destinations), 1) == here
    valid = (dot_last(pick.astype(f32), table) >= 0).astype(f32)
    key = lax.broadcasted_iota(jnp.int32, (slots, total), 1)
    slot = lax.div(lax.rem(key, share_rows), rows) + 1
    mark = (slot == lax.broadcasted_iota(jnp.int32, (slots, total), 0)).astype(f32)
    key = lax.broadcasted_iota(jnp.int32, (tokens, total), 1)
    token = lax.broadcasted_iota(jnp.int32, (tokens, total), 0) + head * tokens
    good = ((key < remote) & (dot(valid, mark) > 0)) | ((key >= remote) & (key - remote <= token))
    masks = jnp.where(good, 0.0, -1e30)
    bias[...] = masks
    tall_masks = jnp.concatenate([masks, jnp.zeros((128 - tokens, total), f32)], axis=0)
    key_bias[...] = tall_masks.T.astype(bf16)


def stage_kernel(local_blocks, sel, fetched, in0, in1, in2, in3, outgoing):
    parts = (in0, in1, in2, in3)
    slots = sel.shape[0]
    rows = fetched.shape[1]
    height = in0.shape[1]
    here = lax.axis_index("seq")
    first = (slots - 1) * rows
    for j in range(1, slots):
        piece = fetched[lax.div(jnp.maximum(sel[j, here], 0), local_blocks)]
        for v in range(len(parts)):
            outgoing[v, (j - 1) * rows : j * rows, :] = piece
    for k in range(len(parts)):
        for v in range(len(parts)):
            at = first + k * height
            outgoing[v, at : at + height, :] = parts[k][v]


def spread_kernel(share, staged, outgoing):
    side = outgoing.shape[0]
    lane_low = (lax.broadcasted_iota(jnp.int32, (share, 128), 1) < 64).astype(f32)
    third, fourth = staged[2, 0:share, :], staged[3, 0:share, :]
    rope = third[:, 256:384] * lane_low.astype(bf16) + fourth[:, 256:384] * (
        1.0 - lane_low
    ).astype(bf16)
    long = share * 2 // 3
    rest = share - long
    for u in range(side):
        outgoing[u, 0:share, :] = staged[0, 0:share, :]
        outgoing[u, share : 2 * share, :] = staged[1, 0:share, :]
        outgoing[u, 2 * share : 3 * share, 0:256] = third[:, 0:256]
        outgoing[u, 2 * share : 3 * share, 256:384] = rope
        at = 3 * share
        outgoing[u, at : at + long, 0:256] = fourth[0:long, 0:256]
        outgoing[u, at : at + rest, 256:384] = fourth[long:, 0:128]
        outgoing[u, at + rest : at + long, 256:384] = fourth[long:, 128:256]


def compute_kernel(
    loss_weight,
    index_scale,
    index_heads,
    staged,
    spread_shares,
    bias,
    key_bias,
    own_rope,
    latent,
    index,
    grad_queries,
    grad_weights,
    shares,
    keys,
    index_k,
    scores,
    highest,
    active,
    slope,
    grad_pre,
    logit_rows,
    target_rows,
    grad_keys,
    sems,
):
    step = staged.shape[0]
    sources = step * step
    groups = sources // 2
    tokens, total = bias.shape
    block = own_rope.shape[0]
    latent_width = latent.shape[1]
    half_width = latent_width // 2
    index_width = index.shape[1]
    query_rows = target_rows.shape[0]
    heads = query_rows // tokens
    index_rows = logit_rows.shape[0]
    remote = total - block
    share_rows = remote // groups
    tile = 2 * 128
    tiles = total // tile
    score_rows = step * query_rows
    chunk = step * index_rows
    height = (staged.shape[1] - share_rows) // step
    tall = height - query_rows
    rest = query_rows - tall
    core, own_u, _ = place(step)
    own_rows = pl.ds(latent.shape[0] - block, block)
    copies = (
        pltpu.make_async_copy(
            latent.at[own_rows], keys.at[pl.ds(remote, block), pl.ds(0, latent_width)], sems.at[0]
        ),
        pltpu.make_async_copy(index.at[own_rows], index_k.at[pl.ds(remote, block)], sems.at[1]),
    )
    for copy in copies:
        copy.start()

    long = share_rows * 2 // 3
    short = share_rows - long
    last = 3 * share_rows
    under = lax.broadcasted_iota(jnp.int32, (share_rows, 128), 1) < 64
    middle_lanes = slice(half_width, latent_width)
    rope_lanes = slice(latent_width, latent_width + 128)

    def gather_keys(g):
        i, u = g // step, g % step
        at = slice(g * share_rows, (g + 1) * share_rows)
        low = slice(i * share_rows, (i + 1) * share_rows)
        keys[at, 0:half_width] = spread_shares[u, low, 0:half_width]
        index_k[at, :] = spread_shares[u, low, half_width:]
        rope = spread_shares[u, 2 * share_rows : last, half_width:].astype(f32)
        swapped = pltpu.roll(rope, 64, 1)
        if i == 0:
            keys[at, middle_lanes] = spread_shares[u, 2 * share_rows : last, 0:half_width]
            keys[at, rope_lanes] = jnp.where(under, rope, swapped).astype(bf16)
        else:
            top = slice(g * share_rows, g * share_rows + long)
            end = slice(g * share_rows + long, (g + 1) * share_rows)
            keys[top, middle_lanes] = spread_shares[u, last : last + long, 0:half_width]
            keys[end, middle_lanes] = jnp.concatenate(
                [
                    spread_shares[u, last : last + short, half_width:],
                    spread_shares[u, last + short : last + long, half_width:],
                ],
                axis=1,
            )
            keys[at, rope_lanes] = jnp.where(under, swapped, rope).astype(bf16)

    keys[remote:total, latent_width : latent_width + 128] = own_rope[...]
    keys[:, latent_width + 128 :] = key_bias[...]
    target_rows[...] = jnp.zeros_like(target_rows)
    logit_rows[...] = jnp.zeros_like(logit_rows)
    for copy in copies:
        copy.wait()

    lane_low = lax.broadcasted_iota(jnp.int32, (query_rows // 2, 128), 1) < 64
    lane_low = lane_low.astype(f32)
    keep_low = lane_low.astype(bf16)
    keep_high = (1.0 - lane_low).astype(bf16)

    on_token = (
        lax.broadcasted_iota(jnp.int32, (query_rows, 128), 0) // heads
        == lax.broadcasted_iota(jnp.int32, (query_rows, 128), 1)
    ).astype(bf16)

    def queries_of(v):
        pieces = []
        for k in range(step):
            at = share_rows + k * height
            below = at + query_rows
            rope = staged[v, below + rest : below + tall, 128:256]
            pieces.append(
                jnp.concatenate(
                    [
                        staged[v, at:below, :],
                        jnp.concatenate(
                            [
                                staged[v, below : below + tall, 0:128],
                                staged[v, below : below + rest, 128:256],
                            ],
                            axis=0,
                        ),
                        jnp.concatenate([rope * keep_low, rope * keep_high], axis=0),
                        on_token,
                    ],
                    axis=1,
                )
            )
        return jnp.concatenate(pieces, axis=0)

    def index_queries_of(v):
        pieces = []
        for k in range(step):
            below = share_rows + k * height + query_rows
            pieces.append(staged[v, below : below + index_rows, 256:384])
        return jnp.concatenate(pieces, axis=0)

    def weights_of(v):
        columns = []
        for k in range(step):
            below = share_rows + k * height + query_rows
            pieces = staged[v, below + index_rows : below + tall, 256:384].astype(f32)
            early = lax.broadcasted_iota(jnp.int32, pieces.shape, 1) < 3
            columns.append(jnp.sum(jnp.where(early, pieces, 0.0), axis=1, keepdims=True))
            columns.append(jnp.sum(jnp.where(early, 0.0, pieces), axis=1, keepdims=True))
        return jnp.concatenate(columns, axis=0).reshape(step, index_rows, 1)

    def source_of(v, k):
        return head_at(step, core, lax.rem(own_u + step - k, step), v)

    tile_at = [slice(k * tile, (k + 1) * tile) for k in range(tiles)]

    def soften(c, state, k):
        score_at = slice(c * score_rows, (c + 1) * score_rows)
        if k == 0:
            state["top"] = jnp.max(state["best"], axis=1, keepdims=True)
            state["sums"] = jnp.zeros((score_rows, 128), f32)
        if k == tiles // 2:
            weight = 1.0 / ((heads * sources) * jnp.sum(state["sums"], axis=1, keepdims=True))
            state["weight"] = weight.reshape(step, query_rows, 1)
        for i in range(2):
            if k < tiles // 2:
                at = tile_at[2 * k + i]
                power = jnp.exp((scores[score_at, at] - state["top"]) * score_scale)
                scores[score_at, at] = power
                state["sums"] = state["sums"] + (power[:, 0:128] + power[:, 128:256])
            else:
                at = tile_at[2 * k - tiles + i]
                power = scores[score_at, at].reshape(step, query_rows, tile)
                target_rows[:, at] += jnp.sum(power * state["weight"], axis=0)

    state = None
    ready = 0
    for c in range(sources // step):
        score_at = slice(c * score_rows, (c + 1) * score_rows)
        rows = slice(c * chunk, (c + 1) * chunk)
        queries = queries_of(c)
        index_q = index_queries_of(c)
        weights = weights_of(c)
        best = jnp.full((score_rows, 128), -3e38, f32)
        for k in range(tiles):
            at = tile_at[k]
            while c == 0 and ready < min((k + 1) * tile, remote):
                gather_keys(ready // share_rows)
                ready += share_rows
            part = dot_last(queries, keys[at, :])
            scores[score_at, at] = part
            best = jnp.maximum(best, jnp.maximum(part[:, 0:128], part[:, 128:256]))
            act, rate = gelu_pair(dot_last(index_q, index_k[at, :]) * index_scale)
            active[rows, at] = act
            slope[rows, at] = rate
            logit_rows[:, at] += jnp.sum(
                act.reshape(step, index_rows, tile) * weights, axis=0
            )
            if state is not None:
                soften(c - 1, state, k)
        state = {"best": best}
    for k in range(tiles):
        soften(sources // step - 1, state, k)

    def gather(count):
        return (
            lax.broadcasted_iota(jnp.int32, (tokens, tokens * count), 1) // count
            == lax.broadcasted_iota(jnp.int32, (tokens, tokens * count), 0)
        ).astype(f32)

    spread = (
        lax.broadcasted_iota(jnp.int32, (index_rows, tokens), 0) // index_heads
        == lax.broadcasted_iota(jnp.int32, (index_rows, tokens), 1)
    ).astype(bf16)
    logits = dot(gather(index_heads), logit_rows[...], lax.Precision.HIGHEST) + bias[...]
    target = dot(gather(heads), target_rows[...], lax.Precision.HIGHEST)
    likely = jnp.exp(logits - jnp.max(logits, axis=1, keepdims=True))
    predicted = likely / jnp.sum(likely, axis=1, keepdims=True)
    grad_logits = jnp.where(
        bias[...] == 0.0, loss_weight * (predicted - target), 0.0
    ).astype(bf16)
    logit_rows[...] = dot(spread, grad_logits)

    for c in range(sources // step):
        rows = slice(c * chunk, (c + 1) * chunk)
        weights = weights_of(c) * index_scale
        sums = jnp.zeros((chunk, 128), f32)
        for k in range(tiles):
            at = slice(k * tile, (k + 1) * tile)
            grad = logit_rows[:, at][None]
            product = (
                active[rows, at].reshape(step, index_rows, tile) * grad
            ).reshape(chunk, tile)
            sums = sums + (product[:, 0:128] + product[:, 128:256])
            grad_pre[rows, at] = (
                (slope[rows, at].reshape(step, index_rows, tile) * (grad * weights))
                .reshape(chunk, tile)
                .astype(bf16)
            )
        turned = jnp.broadcast_to(jnp.sum(sums, axis=1, keepdims=True), (chunk, 128)).T
        for k in range(step):
            own = turned[0:8] if k == 0 else pltpu.roll(turned[0:8], 128 - k * index_rows, 1)
            own_high = own.astype(bf16)
            own_low = (own - own_high.astype(f32)).astype(bf16)
            grad_weights[source_of(c, k)] = jnp.concatenate([own_high, own_low], axis=0)

    result = dot(grad_pre[...], index_k[...]).astype(bf16)
    for v in range(step):
        for k in range(step):
            at = (v * step + k) * index_rows
            grad_queries[source_of(v, k)] = result[at : at + index_rows]
    turned = jnp.concatenate([index_queries_of(v) for v in range(step)], axis=0)
    turned = turned.astype(f32).T.astype(bf16)
    for k in range(tiles):
        at = slice(k * tile, (k + 1) * tile)
        grad_keys[at, :] = dot(turned, grad_pre[:, at]).T
    small = block // sources
    slots = total // block
    for g in range(groups):
        own = grad_keys[remote + g * 2 * small : remote + (g + 1) * 2 * small, :]
        own = own.reshape(1, 2, small, index_width)
        rest_keys = grad_keys[g * share_rows : (g + 1) * share_rows, :]
        rest_keys = rest_keys.reshape(slots - 1, 2, small, index_width)
        both_keys = jnp.concatenate([own, rest_keys], axis=0)
        for i in range(2):
            shares[i * groups + g] = both_keys[:, i].reshape(block, index_width).astype(bf16)


def route_kernel(local_blocks, sel_turned, collected, outgoing, own_sum):
    slots, owners = sel_turned.shape
    total, width = outgoing.shape[0], collected.shape[1]
    small = total // owners
    summed = collected[0].astype(f32)
    for k in range(1, collected.shape[0]):
        summed = summed + collected[k].astype(f32)
    own_sum[...] = summed[0:small]
    here = lax.axis_index("seq")
    pick = (lax.broadcasted_iota(jnp.int32, (total, owners), 1) == here).astype(f32)
    blocks = dot_last(pick, sel_turned[...].astype(f32))
    slot = lax.broadcasted_iota(jnp.int32, (slots, width), 1) // small
    mark = (slot == lax.broadcasted_iota(jnp.int32, (slots, width), 0)).astype(f32)
    block = dot(blocks, mark)
    row = lax.broadcasted_iota(jnp.int32, (total, width), 0)
    column = lax.broadcasted_iota(jnp.int32, (total, width), 1)
    first = (row // small * local_blocks).astype(f32)
    chosen = (block >= first) & (block < first + local_blocks)
    chosen = chosen & (column >= small) & (column % small == row % small)
    outgoing[...] = dot(chosen.astype(bf16), summed.astype(bf16)).astype(bf16)


def last_kernel(groups, index_heads, final, grad_queries, grad_weights, grad_keys):
    sources, _, width = final.shape
    block = grad_weights.shape[1]
    tokens = block // sources
    index_rows = tokens * index_heads
    local_blocks = grad_keys.shape[0] // block
    small = block // sources
    own_rows = local_blocks * small
    second = own_rows + index_rows
    for k in range(sources):
        part = final[k, 0:own_rows, :].astype(f32)
        half, group = k // groups, k % groups
        for j in range(local_blocks):
            at = j * block + group * 2 * small + half * small
            grad_keys[at : at + small, :] = part[j * small : (j + 1) * small]
        grad_queries[k * index_rows : (k + 1) * index_rows, :] = final[
            k, own_rows:second, :
        ].astype(f32)
    row = lax.broadcasted_iota(jnp.int32, (block, width), 0)
    lane = lax.broadcasted_iota(jnp.int32, (block, width), 1)
    keep = (lane < index_rows) & (lax.div(lane, index_heads) == row % tokens)
    which = lax.broadcasted_iota(jnp.int32, (8, width), 0)
    head = lax.rem(lax.broadcasted_iota(jnp.int32, (8, width), 1), index_heads)
    fold = (which == head).astype(bf16)
    result = jnp.zeros((8, block), f32)
    for i in range(2):
        lines = []
        for k in range(sources):
            whole = final[k, second : second + 16, :].astype(f32)
            lines.append(jnp.broadcast_to(whole[8 * i : 8 * i + 1], (tokens, width)))
        lines = jnp.concatenate(lines, axis=0)
        result = result + dot_last(fold, jnp.where(keep, lines, 0.0).astype(bf16))
    grad_weights[...] = result[0:index_heads]


def exchange(array, axis, groups=None):
    return lax.all_to_all(
        array, axis, split_axis=0, concat_axis=0, tiled=True, axis_index_groups=groups
    )


def exchange_alone(array, axis, others, groups=None):
    array, others = lax.optimization_barrier((array, others))
    return lax.optimization_barrier((exchange(array, axis, groups), others))


def flat_index(side, seq_count, u, v, seq):
    x, y = (v, u) if seq % 2 == 0 else (u, v)
    return (x * side + y) * seq_count + seq


def lines(side, seq_count, along_u):
    return [
        [
            flat_index(side, seq_count, *((i, j) if along_u else (j, i)), seq)
            for i in range(side)
        ]
        for seq in range(seq_count)
        for j in range(side)
    ]


def shift_along_u(side, seq_count, k):
    return [
        (
            flat_index(side, seq_count, u, v, seq),
            flat_index(side, seq_count, (u + k) % side, v, seq),
        )
        for seq in range(seq_count)
        for u in range(side)
        for v in range(side)
    ]


def pad_lanes(array, width):
    return jnp.pad(array, [(0, 0)] * (array.ndim - 1) + [(0, width - array.shape[-1])])


def body(
    q_latent, q_rope, latent_cache, rope_keys, index_queries, index_weights, index_keys, sel_blocks
):
    head_count = lax.axis_size("head")
    seq_count = lax.axis_size("seq")
    head_index = lax.axis_index("head")
    seq_index = lax.axis_index("seq")
    block, heads, latent_width = q_latent.shape
    rope_width = q_rope.shape[2]
    index_heads, index_width = index_queries.shape[1:]
    slot_count = sel_blocks.shape[1]
    local_blocks = latent_cache.shape[0] // block
    index_scale = index_width ** (-0.5)
    loss_weight = float(slot_count * block)
    groups = head_count // 2
    side = math.isqrt(head_count)
    rows = block // groups
    small = rows // 2
    tokens = block // head_count
    half_width = latent_width // 2
    lanes = half_width + index_width
    remote_slots = slot_count - 1

    later = sel_blocks[:, 1:]
    offsets = later - seq_index * local_blocks
    inside = (later >= 0) & (offsets >= 0) & (offsets < local_blocks)
    wanted = jnp.any(inside, axis=1)
    which = jnp.sum(jnp.where(inside, offsets, 0), axis=1)
    in_vmem = pl.BlockSpec(memory_space=pltpu.VMEM)
    in_smem = pl.BlockSpec(memory_space=pltpu.SMEM)
    in_place = pl.BlockSpec(memory_space=pl.ANY)

    packed = pl.pallas_call(
        functools.partial(first_kernel, groups),
        out_shape=jax.ShapeDtypeStruct((seq_count * rows, lanes), bf16),
        in_specs=[in_place] * 4,
        out_specs=in_vmem,
        scratch_shapes=[
            pltpu.VMEM((2, local_blocks, rows, latent_width), bf16),
            pltpu.VMEM((2, local_blocks, rows, index_width), bf16),
            pltpu.VMEM((rope_width, local_blocks * block), bf16),
            pltpu.VMEM((slot_count, seq_count), jnp.int32),
            pltpu.SemaphoreType.DMA((6,)),
        ],
        compiler_params=pltpu.CompilerParams(vmem_limit_bytes=60 * 1024 * 1024),
    )(
        sel_blocks.T,
        latent_cache.reshape(local_blocks, block, latent_width),
        rope_keys.T,
        index_keys.reshape(local_blocks, block, index_width),
    )
    fetched = exchange(packed.reshape(seq_count, rows, lanes), "seq")

    share_rows = remote_slots * rows
    query_rows = tokens * heads
    index_rows = tokens * index_heads
    latent_parts = q_latent.reshape(block * heads, latent_width)
    rope_parts = q_rope.reshape(head_count, 2, query_rows // 2, rope_width)
    rope_parts = jnp.concatenate([rope_parts[:, 0], rope_parts[:, 1]], axis=-1)
    rope_parts = rope_parts.reshape(head_count * query_rows // 2, 2 * rope_width)
    index_parts = index_queries.reshape(head_count * index_rows, index_width)
    weight_parts = index_weights.reshape(head_count, 2, index_rows // 2, 1)
    high = lax.reduce_precision(weight_parts, 8, 7)
    middle = lax.reduce_precision(weight_parts - high, 8, 7)
    low = weight_parts - high - middle
    pieces = jnp.concatenate([high, middle, low], axis=-1).astype(bf16)
    pieces = pad_lanes(jnp.concatenate([pieces[:, 0], pieces[:, 1]], axis=-1), 128)
    pieces = pieces.reshape(head_count * index_rows // 2, 128)
    height = query_rows + index_rows + index_rows // 2
    own_rope = rope_keys[(local_blocks - 1) * block :]
    own_rope = jnp.concatenate([own_rope, own_rope], axis=-1)
    total = slot_count * block
    axes = ("head", "seq")
    *parts, bias, key_bias = pl.pallas_call(
        functools.partial(query_kernel, side, groups),
        out_shape=tuple([jax.ShapeDtypeStruct((side, height, lanes), bf16)] * side)
        + (
            jax.ShapeDtypeStruct((tokens, total), f32),
            jax.ShapeDtypeStruct((total, 128), bf16),
        ),
        in_specs=[in_vmem] * 5,
        out_specs=tuple([in_vmem] * (side + 2)),
        compiler_params=pltpu.CompilerParams(vmem_limit_bytes=24 * 1024 * 1024),
    )(sel_blocks.T, latent_parts, rope_parts, index_parts, pieces)
    for k in range(1, side):
        parts[k] = lax.ppermute(parts[k], axes, shift_along_u(side, seq_count, k))
    outgoing = pl.pallas_call(
        functools.partial(stage_kernel, local_blocks),
        out_shape=jax.ShapeDtypeStruct((side, share_rows + side * height, lanes), bf16),
        in_specs=[in_smem] + [in_vmem] * (side + 1),
        out_specs=in_vmem,
        compiler_params=pltpu.CompilerParams(vmem_limit_bytes=24 * 1024 * 1024),
    )(sel_blocks.T, fetched, *parts)
    owner = wanted[:, None] & (which[:, None] == jnp.arange(local_blocks)[None, :])
    owner = owner.astype(f32)
    later = (bias, key_bias, own_rope, owner)
    staged, later = exchange_alone(outgoing, axes, later, lines(side, seq_count, False))
    spread = pl.pallas_call(
        functools.partial(spread_kernel, share_rows),
        out_shape=jax.ShapeDtypeStruct((side, share_rows * 11 // 3, lanes), bf16),
        in_specs=[in_vmem],
        out_specs=in_vmem,
        compiler_params=pltpu.CompilerParams(vmem_limit_bytes=16 * 1024 * 1024),
    )(staged)
    spread, (staged, bias, key_bias, own_rope, owner) = exchange_alone(
        spread, axes, (staged, *later), lines(side, seq_count, True)
    )

    all_rows = head_count * index_rows
    grad_queries, grad_weights, shares = pl.pallas_call(
        functools.partial(compute_kernel, loss_weight, index_scale, index_heads),
        out_shape=(
            jax.ShapeDtypeStruct((head_count, index_rows, index_width), bf16),
            jax.ShapeDtypeStruct((head_count, 16, 128), bf16),
            jax.ShapeDtypeStruct((head_count, slot_count * small, index_width), bf16),
        ),
        in_specs=[in_vmem] * 5 + [in_place] * 2,
        out_specs=(in_vmem, in_vmem, in_vmem),
        scratch_shapes=[
            pltpu.VMEM((total, latent_width + 256), bf16),
            pltpu.VMEM((total, index_width), bf16),
            pltpu.VMEM((head_count * query_rows, total), f32),
            pltpu.VMEM((head_count * query_rows, 128), f32),
            pltpu.VMEM((all_rows, total), f32),
            pltpu.VMEM((all_rows, total), f32),
            pltpu.VMEM((all_rows, total), bf16),
            pltpu.VMEM((index_rows, total), f32),
            pltpu.VMEM((query_rows, total), f32),
            pltpu.VMEM((total, index_width), f32),
            pltpu.SemaphoreType.DMA((2,)),
        ],
        compiler_params=pltpu.CompilerParams(vmem_limit_bytes=36 * 1024 * 1024),
    )(
        staged,
        spread,
        bias,
        key_bias,
        own_rope,
        latent_cache,
        index_keys,
    )

    collected, (grad_queries, grad_weights, owner) = exchange_alone(
        shares, "head", (grad_queries, grad_weights, owner)
    )
    routed, own_sum = pl.pallas_call(
        functools.partial(route_kernel, local_blocks),
        out_shape=(
            jax.ShapeDtypeStruct((seq_count * small, index_width), bf16),
            jax.ShapeDtypeStruct((small, index_width), f32),
        ),
        in_specs=[in_vmem, in_vmem],
        out_specs=(in_vmem, in_vmem),
        compiler_params=pltpu.CompilerParams(vmem_limit_bytes=16 * 1024 * 1024),
    )(sel_blocks.T, collected)
    returned, (own_sum, grad_queries, grad_weights, owner) = exchange_alone(
        routed.reshape(seq_count, small, index_width),
        "seq",
        (own_sum, grad_queries, grad_weights, owner),
    )
    owned = jnp.sum(owner[:, :, None, None] * returned.astype(f32)[:, None], axis=0)
    owned = owned.at[local_blocks - 1].add(own_sum)

    own_rows = local_blocks * small
    last = jnp.concatenate(
        [
            jnp.broadcast_to(
                owned.reshape(own_rows, index_width).astype(bf16), (head_count, own_rows, index_width)
            ),
            grad_queries,
            grad_weights,
        ],
        axis=1,
    )
    final, _ = exchange_alone(last, "head", ())
    out_queries, out_weights, grad_keys = pl.pallas_call(
        functools.partial(last_kernel, groups, index_heads),
        out_shape=(
            jax.ShapeDtypeStruct((block * index_heads, index_width), f32),
            jax.ShapeDtypeStruct((index_heads, block), f32),
            jax.ShapeDtypeStruct((local_blocks * block, index_width), f32),
        ),
        in_specs=[in_vmem],
        out_specs=(in_vmem, in_vmem, in_vmem),
        compiler_params=pltpu.CompilerParams(vmem_limit_bytes=16 * 1024 * 1024),
    )(final)
    return (out_queries.reshape(block, index_heads, index_width), out_weights.T, grad_keys)


def solution(mesh):
    placed = (
        P("seq", "head", None),
        P("seq", "head", None),
        P("seq", None),
        P("seq", None),
        P("seq", "head", None),
        P("seq", "head"),
        P("seq", None),
        P(),
    )
    return jax.shard_map(
        body,
        mesh=mesh,
        in_specs=placed,
        out_specs=(P("seq", "head", None), P("seq", "head"), P("seq", None)),
        check_vma=False,
    )
```
